512 devices in a mesh: tok: 8 (over z), row: 8 (over x, core), col: 8 (over y).
Axes of the slice: x: 4, y: 8, z: 8, core: 2. Of those that a mesh axis runs over, the one named last changes fastest.
Arguments:
- tokens: bfloat16 [576, 8192], P('tok', ('row', 'col')), may hold values from -50 to 50
- d_out: bfloat16 [576, 8192], P('tok', ('row', 'col')), may hold values from -25 to 25
- gain: bfloat16 [8192], P(('row', 'col')), may hold values from 0.3984375 to 2.5
- gate_weight: bfloat16 [14336, 8192], P(('tok', 'col'), 'row'), may hold values from -0.0625 to 0.0625
- up_weight: bfloat16 [14336, 8192], P(('tok', 'col'), 'row'), may hold values from -0.0625 to 0.0625
- down_weight: bfloat16 [14336, 8192], P(('tok', 'col'), 'row'), may hold values from -0.046875 to 0.046875
Outputs:
- d_tokens: bfloat16 [576, 8192], P('tok', ('row', 'col'))
- d_gain: float32 [8192], P(('row', 'col'))
- d_down: bfloat16 [14336, 8192], P(('tok', 'col'), 'row')
The draws below stay inside these ranges and needn't reach their ends.
All inputs are finite; a program needn't handle non-finite values.
Results may differ from the reference program's by a relative error of at most 0.007.
Values may be sent and summed in bfloat16 or wider, within the bound.
No kernel may reach another device: no remote copies, remote signals or barrier semaphores. Data moves between devices by JAX's collectives and lax.ppermute only.
A program may use at most 64 MiB of HBM per device.

```python
import math
import jax
import jax.numpy as jnp
from jax import lax

D = 8192
FF = 14336
TOK_DEV = 72
TOKENS = 576
N_TOK = 8


def scale_table(key, rows, cols):
    first, second = jax.random.split(key)
    row_scale = 10.0 ** (0.5 * jnp.arange(rows, dtype=jnp.float32) / rows + 0.5 * jax.random.uniform(first, (rows,)))
    col_scale = 10.0 ** (0.5 * jnp.arange(cols, dtype=jnp.float32) / cols + 0.5 * jax.random.uniform(second, (cols,)))
    return row_scale[:, None] * col_scale[None, :]


def draw_tokens(key, part):
    key = jax.random.fold_in(key, 11)
    first, second = jax.random.split(key)
    scales = scale_table(first, TOKENS, D)
    base = jnp.clip(jax.random.normal(second, (TOKENS, D)), -5.0, 5.0)
    return (0.1 * base * scales).astype(jnp.bfloat16)


def draw_d_out(key, part):
    key = jax.random.fold_in(key, 23)
    first, second = jax.random.split(key, 2)
    scales = scale_table(first, TOKENS, D)
    base = jnp.clip(jax.random.normal(second, (TOKENS, D)), -5.0, 5.0)
    return (0.05 * base * scales).astype(jnp.bfloat16)


def steps_of(rng, dims, shards, low, high):
    level, own = 1.0, jax.random.fold_in(rng, 6)
    for axis_at, blocks in shards:
        steps = jnp.exp(jax.random.uniform(jax.random.fold_in(own, axis_at), (blocks,), jnp.float32, low / len(shards), high / len(shards)))
        level = level * jnp.repeat(steps, dims[axis_at] // blocks).reshape([-1 if axis == axis_at else 1 for axis in range(len(dims))])
    return level


def noise(key, extent, spread, limit, shards=(), kind=jnp.bfloat16):
    entries = jax.random.normal(key, extent, jnp.float32) * spread
    if len(shards) > 0:
        entries = steps_of(key, extent, shards, -0.22, 0.18) * entries
    return jnp.clip(entries, min=-limit, max=limit).astype(kind)


def setup_inputs(seed: int = 0) -> dict:
    key_of = jax.random.split(jax.random.key(seed), 7)
    return {
        "tokens": draw_tokens(jax.random.fold_in(key_of[6], 71), 0),
        "d_out": draw_d_out(jax.random.fold_in(key_of[6], 71), 0),
        "gain": jnp.clip(jnp.exp(math.log(2.5) - 1.8364954 * jax.random.uniform(key_of[2], (D,), jnp.float32) ** steps_of(key_of[2], (D,), ((0, 64),), -0.2, 0.2)), 0.3984375, 2.5).astype(jnp.bfloat16),
        "gate_weight": noise(key_of[3], (FF, D), D ** -0.5, 0.0625, ((0, 64), (1, 8))),
        "up_weight": noise(key_of[4], (FF, D), D ** -0.5, 0.0625, ((0, 64), (1, 8))),
        "down_weight": noise(key_of[5], (FF, D), FF ** -0.5, 0.046875, ((0, 64), (1, 8))),
    }


epsilon = 1e-05

def reference(tokens, d_out, gain, gate_weight, up_weight, down_weight):
    inputs = tokens.astype(jnp.float32)
    gain_wide = gain.astype(jnp.float32)
    squares = lax.optimization_barrier(jnp.sum(inputs * inputs, axis=1))
    inv_rms = lax.rsqrt(squares / D + epsilon)
    normed = (inputs * inv_rms[:, None] * gain_wide).astype(jnp.bfloat16)
    gate = jnp.dot(normed, gate_weight.T, preferred_element_type=jnp.float32)
    up_proj = jnp.dot(normed, up_weight.T, preferred_element_type=jnp.float32)
    hidden_grad = jnp.dot(d_out, down_weight.T, preferred_element_type=jnp.float32)
    gate_sig = jax.nn.sigmoid(gate)
    hidden = (gate * gate_sig * up_proj).astype(jnp.bfloat16)
    gate_grad = (hidden_grad * up_proj * gate_sig * (1.0 + gate * (1.0 - gate_sig))).astype(jnp.bfloat16)
    up_grad = (hidden_grad * gate * gate_sig).astype(jnp.bfloat16)

    def add_block(running, start):
        hidden_block = lax.dynamic_slice_in_dim(hidden, start, TOK_DEV, 0)
        grad_block = lax.dynamic_slice_in_dim(d_out, start, TOK_DEV, 0)
        block_term = jnp.dot(hidden_block.T, grad_block, preferred_element_type=jnp.float32)
        rounded = lax.optimization_barrier(block_term.astype(jnp.bfloat16))
        return (running + rounded.astype(jnp.float32), None)
    starts = (jnp.arange(N_TOK) * TOK_DEV).astype(jnp.int32)
    down_sum, _ = lax.scan(add_block, jnp.zeros((FF, D), jnp.float32), starts)
    normed_grad = jnp.dot(gate_grad, gate_weight, preferred_element_type=jnp.float32)
    normed_grad = normed_grad + jnp.dot(up_grad, up_weight, preferred_element_type=jnp.float32)
    scaled = inputs * inv_rms[:, None]
    weighted = normed_grad * gain_wide
    inner = lax.optimization_barrier(jnp.sum(weighted * scaled, axis=1)) / D
    d_tokens = (d_out.astype(jnp.float32) + inv_rms[:, None] * (weighted - scaled * inner[:, None])).astype(jnp.bfloat16)
    d_gain = lax.optimization_barrier(jnp.sum(normed_grad * scaled, axis=0))
    return (d_tokens, d_gain, down_sum.astype(jnp.bfloat16))
```

```python
import jax
import jax.numpy as jnp
from jax import lax
from jax.sharding import PartitionSpec as P

epsilon = 1e-05
F32 = jnp.float32
BF16 = jnp.bfloat16
AXES = ("tok", "row", "col")


def split_wide(value):
    high = lax.reduce_precision(value, 8, 7)
    return high.astype(BF16), (value - high).astype(BF16)


def mixed_groups(tok_count, row_count, col_count, even_along_tok):
    groups = []
    for row in range(row_count):
        if (row % 2 == 0) == even_along_tok:
            for col in range(col_count):
                groups.append([(tok * row_count + row) * col_count + col for tok in range(tok_count)])
        else:
            for tok in range(tok_count):
                groups.append([(tok * row_count + row) * col_count + col for col in range(col_count)])
    return groups


def gather_stage(block, count, groups):
    copies = jnp.broadcast_to(block[None], (count,) + block.shape)
    return lax.all_to_all(copies, AXES, 0, 0, tiled=True, axis_index_groups=groups)


def pad_columns(value, extras=()):
    rows, width = value.shape
    parts = [value.astype(BF16)] + [e.reshape(rows, 1).astype(BF16) for e in extras]
    total = width + len(extras)
    goal = -(-total // 128) * 128
    parts.append(jnp.zeros((rows, goal - total), BF16))
    return jnp.concatenate(parts, axis=1)


def on_device(tokens, d_out, gain, gate_weight, up_weight, down_weight):
    nt, nr, nc = (lax.axis_size(a) for a in AXES)
    rows, feats = tokens.shape
    hidden_count = gate_weight.shape[0]
    width = nc * feats
    model = nr * width
    odd = lax.rem(lax.axis_index("row"), 2) == 1

    block = jnp.concatenate([tokens, d_out, jnp.broadcast_to(gain[None], (8, feats))], axis=0)
    stage = gather_stage(block, nc, mixed_groups(nt, nr, nc, False))
    stage = gather_stage(stage, nt, mixed_groups(nt, nr, nc, True))
    stage = jnp.where(odd, jnp.swapaxes(stage, 0, 1), stage)
    tokens_all = jnp.swapaxes(stage[:, :, :rows], 1, 2).reshape(nt * rows, width)
    grad_all = jnp.swapaxes(stage[:, :, rows : 2 * rows], 1, 2).reshape(nt * rows, width)
    gain_all = stage[0, :, 2 * rows].reshape(width)

    wide = tokens_all.astype(F32)
    squares_part = jnp.sum(wide * wide, axis=1)
    scaled_in = (wide * gain_all.astype(F32)).astype(BF16)
    gate_part = jnp.einsum("td,fd->tf", scaled_in, gate_weight, preferred_element_type=F32)
    up_part = jnp.einsum("td,fd->tf", scaled_in, up_weight, preferred_element_type=F32)
    back_part = jnp.einsum("td,fd->tf", grad_all, down_weight, preferred_element_type=F32)
    sums = jnp.concatenate(
        [pad_columns(gate_part, split_wide(squares_part)), pad_columns(up_part), pad_columns(back_part)], axis=1
    )
    slot = sums.shape[1] // 3
    sums = lax.all_to_all(sums.reshape(nr, rows, 3 * slot), "row", 0, 0, tiled=True)
    sums = jnp.sum(sums.astype(F32), axis=0)
    squares = sums[:, hidden_count] + sums[:, hidden_count + 1]
    inv_rms = lax.rsqrt(squares / model + epsilon)
    gate = sums[:, :hidden_count] * inv_rms[:, None]
    up_proj = sums[:, slot : slot + hidden_count] * inv_rms[:, None]
    hidden_grad = sums[:, 2 * slot : 2 * slot + hidden_count]
    gate_sig = jax.nn.sigmoid(gate)
    hidden = (gate * gate_sig * up_proj).astype(BF16)
    gate_grad = (hidden_grad * up_proj * gate_sig * (1.0 + gate * (1.0 - gate_sig))).astype(BF16)
    up_grad = (hidden_grad * gate * gate_sig).astype(BF16)
    inner_part = jnp.sum(gate_grad.astype(F32) * gate + up_grad.astype(F32) * up_proj, axis=1)
    packed = jnp.concatenate(
        [
            pad_columns(hidden, split_wide(inner_part) + split_wide(inv_rms)),
            pad_columns(gate_grad),
            pad_columns(up_grad),
        ],
        axis=1,
    )
    packed = lax.all_gather(packed, "row", axis=0, tiled=True)
    hidden_all = packed[:, :hidden_count]
    gate_grad_all = packed[:, slot : slot + hidden_count]
    up_grad_all = packed[:, 2 * slot : 2 * slot + hidden_count]
    inner_rows = packed[:, hidden_count : hidden_count + 2]
    inv_pair = packed[:, hidden_count + 2 : hidden_count + 4].astype(F32)
    inv_all = inv_pair[:, 0] + inv_pair[:, 1]

    input_term = jnp.einsum("tf,fd->td", gate_grad_all, gate_weight, preferred_element_type=F32)
    input_term = input_term + jnp.einsum("tf,fd->td", up_grad_all, up_weight, preferred_element_type=F32)
    gain_term = jnp.sum(input_term * wide * inv_all[:, None], axis=0)
    d_down = jnp.einsum("tf,td->fd", hidden_all, grad_all, preferred_element_type=F32).astype(BF16)

    inner_rows = jnp.swapaxes(inner_rows.reshape(nt, 1, rows, 2), 2, 3)
    inner_rows = jnp.pad(inner_rows, ((0, 0), (0, 0), (0, 0), (0, feats - rows)))
    gain_rows = jnp.stack(split_wide(gain_term)).reshape(2, nc, feats).swapaxes(0, 1)[None]
    blocks = jnp.concatenate(
        [
            jnp.swapaxes(input_term.astype(BF16).reshape(nt, rows, nc, feats), 1, 2),
            jnp.broadcast_to(inner_rows, (nt, nc, 2, feats)),
            jnp.broadcast_to(gain_rows, (nt, nc, 2, feats)),
            jnp.zeros((nt, nc, 4, feats), BF16),
        ],
        axis=2,
    )
    blocks = lax.all_to_all(blocks.reshape(nt * nc, rows + 8, feats), ("tok", "col"), 0, 0, tiled=True)
    total = jnp.sum(blocks.astype(F32), axis=0)
    normed_grad = total[:rows]
    inner = (total[rows, :rows] + total[rows + 1, :rows]) / model
    d_gain = total[rows + 2] + total[rows + 3]
    inv_own = lax.dynamic_slice_in_dim(inv_all, lax.axis_index("tok") * rows, rows)[:, None]
    scaled = tokens.astype(F32) * inv_own
    weighted = normed_grad * gain.astype(F32)
    d_tokens = (d_out.astype(F32) + inv_own * (weighted - scaled * inner[:, None])).astype(BF16)
    return (d_tokens, d_gain, d_down)


def solution(mesh):
    placed = (
        P("tok", ("row", "col")),
        P("tok", ("row", "col")),
        P(("row", "col")),
        P(("tok", "col"), "row"),
        P(("tok", "col"), "row"),
        P(("tok", "col"), "row"),
    )
    return jax.shard_map(
        on_device,
        mesh=mesh,
        in_specs=placed,
        out_specs=(P("tok", ("row", "col")), P(("row", "col")), P(("tok", "col"), "row")),
        check_vma=False,
    )
```

```python
import functools

import jax
import jax.numpy as jnp
from jax import lax
from jax.experimental import pallas as pl
from jax.experimental.pallas import tpu as pltpu
from jax.sharding import PartitionSpec as P

epsilon = 1e-05
F32 = jnp.float32
BF16 = jnp.bfloat16
AXES = ("tok", "row", "col")
SLOT = 256
EXTRA = 8
NT_DIMS = (((1,), (1,)), ((), ()))
PARAMS = pltpu.CompilerParams(vmem_limit_bytes=40 * 1024 * 1024)


def split_wide(value):
    high = value.astype(BF16).astype(F32)
    return high, value - high


def mixed_groups(tok_count, row_count, col_count, even_along_tok):
    groups = []
    for row in range(row_count):
        if (row % 2 == 0) == even_along_tok:
            for col in range(col_count):
                groups.append([(tok * row_count + row) * col_count + col for tok in range(tok_count)])
        else:
            for tok in range(tok_count):
                groups.append([(tok * row_count + row) * col_count + col for col in range(col_count)])
    return groups


def gather_stage(block, count, groups):
    copies = jnp.broadcast_to(block[None], (count,) + block.shape)
    return lax.all_to_all(copies, AXES, 0, 0, tiled=True, axis_index_groups=groups)


def block_pair(ref, odd, pair, col, nt, nc, rows):
    out = []
    for tok in (2 * pair, 2 * pair + 1):
        at = jnp.where(odd, col * nt + tok, tok * nc + col)
        out.append(ref[at].astype(F32))
    joined = jnp.concatenate([out[0][:rows], out[1][:rows]], axis=0)
    return joined, out[0]


def padded_weight(ref, scratch):
    count = ref.shape[0]
    scratch[:count, :] = ref[...]
    scratch[count:, :] = jnp.zeros((scratch.shape[0] - count, ref.shape[1]), BF16)
    return scratch[...]


def up_kernel(nt, nc, rows, odd_ref, blocks_ref, gate_ref, up_ref, part_ref, tokens_ref, scaled_ref, w_ref):
    odd = odd_ref[0] == 1
    count, feats = gate_ref.shape[0], blocks_ref.shape[2]
    totals = []
    for pair in range(nt // 2):
        at = pl.ds(pair * 2 * rows, 2 * rows)
        squares = jnp.zeros((2 * rows, feats), F32)
        for col in range(nc):
            wide, first = block_pair(blocks_ref, odd, pair, col, nt, nc, rows)
            cols = pl.ds(col * feats, feats)
            tokens_ref[at, cols] = wide.astype(BF16)
            scaled_ref[at, cols] = (wide * first[rows : rows + 1]).astype(BF16)
            squares = squares + wide * wide
        totals.append(jnp.sum(squares, axis=1, keepdims=True))
    high, low = split_wide(jnp.concatenate(totals, axis=0))
    scaled = scaled_ref[...]
    gate = lax.dot_general(scaled, padded_weight(gate_ref, w_ref.at[0]), NT_DIMS, preferred_element_type=F32)
    lane = lax.broadcasted_iota(jnp.int32, gate.shape, 1)
    gate = jnp.where(lane == count, high, jnp.where(lane == count + 1, low, gate))
    up = lax.dot_general(scaled, padded_weight(up_ref, w_ref.at[1]), NT_DIMS, preferred_element_type=F32)
    for tok in range(nt):
        part_ref[tok, :, :SLOT] = gate[tok * rows : (tok + 1) * rows].astype(BF16)
        part_ref[tok, :, SLOT:] = up[tok * rows : (tok + 1) * rows].astype(BF16)


def back_kernel(nt, nc, rows, odd_ref, blocks_ref, down_ref, part_ref, grads_ref, w_ref):
    odd = odd_ref[0] == 1
    feats = blocks_ref.shape[2]
    for pair in range(nt // 2):
        at = pl.ds(pair * 2 * rows, 2 * rows)
        for col in range(nc):
            wide, _ = block_pair(blocks_ref, odd, pair, col, nt, nc, rows)
            grads_ref[at, pl.ds(col * feats, feats)] = wide.astype(BF16)
    back = lax.dot_general(
        grads_ref[...], padded_weight(down_ref, w_ref), NT_DIMS, preferred_element_type=F32
    )
    for tok in range(nt):
        part_ref[tok] = back[tok * rows : (tok + 1) * rows].astype(BF16)


def swiglu_kernel(model, count, forward_ref, back_ref, packed_ref):
    sums = jnp.sum(forward_ref[...].astype(F32), axis=0)
    hidden_grad = jnp.sum(back_ref[...].astype(F32), axis=0)
    gate, up_proj = sums[:, :SLOT], sums[:, SLOT:]
    lane = lax.broadcasted_iota(jnp.int32, gate.shape, 1)
    at_squares = (lane >= count) & (lane < count + 2)
    squares = jnp.sum(jnp.where(at_squares, gate, 0.0), axis=1, keepdims=True)
    inv_rms = lax.rsqrt(squares / model + epsilon)
    gate = jnp.where(lane < count, gate * inv_rms, 0.0)
    up_proj = up_proj * inv_rms
    sig = jax.nn.sigmoid(gate)
    hidden = gate * sig * up_proj
    gate_grad = (hidden_grad * up_proj * sig * (1.0 + gate * (1.0 - sig))).astype(BF16)
    up_grad = (hidden_grad * gate * sig).astype(BF16)
    inner = jnp.sum(gate_grad.astype(F32) * gate + up_grad.astype(F32) * up_proj, axis=1, keepdims=True)
    for place, value in enumerate(split_wide(inner) + split_wide(inv_rms)):
        hidden = jnp.where(lane == count + place, value, hidden)
    packed_ref[:, :SLOT] = hidden.astype(BF16)
    packed_ref[:, SLOT : 2 * SLOT] = gate_grad
    packed_ref[:, 2 * SLOT :] = up_grad


def input_kernel(nt, rows, feats, count, packed_ref, gate_ref, up_ref, tokens_ref, out_ref, inv_ref, extra_ref):
    base = count % 128

    @pl.when(pl.program_id(0) == 0)
    def _():
        tail = packed_ref[:, SLOT - 128 : SLOT].astype(F32)
        lane = lax.broadcasted_iota(jnp.int32, tail.shape, 1)
        at_inv = (lane >= base + 2) & (lane < base + 4)
        inv_ref[...] = jnp.sum(jnp.where(at_inv, tail, 0.0), axis=1, keepdims=True)
        for tok in range(nt):
            piece = tail[tok * rows : (tok + 1) * rows]
            square = jnp.concatenate([piece, jnp.zeros((128 - rows, 128), F32)], axis=0)
            extra_ref[tok] = square.T[base : base + EXTRA]

    fill = jnp.zeros((SLOT - count, gate_ref.shape[1]), BF16)
    term = jnp.dot(
        packed_ref[:, SLOT : 2 * SLOT],
        jnp.concatenate([gate_ref[...], fill], axis=0),
        preferred_element_type=F32,
    )
    term = term + jnp.dot(
        packed_ref[:, 2 * SLOT :],
        jnp.concatenate([up_ref[...], fill], axis=0),
        preferred_element_type=F32,
    )
    gain_term = jnp.sum(term * (tokens_ref[...].astype(F32) * inv_ref[...]), axis=0, keepdims=True)
    high, low = split_wide(gain_term)
    spot = lax.broadcasted_iota(jnp.int32, (EXTRA, feats), 0)
    for part in range(gate_ref.shape[1] // feats):
        cols = slice(part * feats, (part + 1) * feats)
        for tok in range(nt):
            extra = jnp.where(spot == 2, high[:, cols], jnp.where(spot == 3, low[:, cols], extra_ref[tok]))
            block = jnp.concatenate([term[tok * rows : (tok + 1) * rows, cols], extra], axis=0)
            out_ref[tok, part] = block.astype(BF16)


def whole(memory=pltpu.VMEM):
    return pl.BlockSpec(memory_space=memory)


def on_device(tokens, d_out, gain, gate_weight, up_weight, down_weight):
    nt, nr, nc = (lax.axis_size(a) for a in AXES)
    rows, feats = tokens.shape
    count = gate_weight.shape[0]
    width = nc * feats
    model = nr * width
    odd = lax.rem(lax.axis_index("row"), 2)
    odd_flag = odd.reshape(1).astype(jnp.int32)

    block = jnp.concatenate([tokens, jnp.broadcast_to(gain[None], (EXTRA, feats)), d_out], axis=0)
    stage = gather_stage(block, nc, mixed_groups(nt, nr, nc, False))
    second = mixed_groups(nt, nr, nc, True)
    tall = rows + EXTRA
    token_blocks = gather_stage(stage[:, :tall], nt, second).reshape(nt * nc, tall, feats)
    grad_blocks = gather_stage(stage[:, tall:], nt, second).reshape(nt * nc, rows, feats)

    flops = 2 * nt * rows * width * SLOT
    forward, tokens_all = pl.pallas_call(
        functools.partial(up_kernel, nt, nc, rows),
        out_shape=(
            jax.ShapeDtypeStruct((nt, rows, 2 * SLOT), BF16),
            jax.ShapeDtypeStruct((nt * rows, width), BF16),
        ),
        in_specs=[whole(pltpu.SMEM)] + [whole()] * 3,
        out_specs=(whole(), whole()),
        scratch_shapes=[pltpu.VMEM((nt * rows, width), BF16), pltpu.VMEM((2, SLOT, width), BF16)],
        compiler_params=PARAMS,
        cost_estimate=pl.CostEstimate(flops=2 * flops, bytes_accessed=4 * nt * rows * width, transcendentals=0),
        name="gate_up_parts",
    )(odd_flag, token_blocks, gate_weight, up_weight)
    back, grad_all = pl.pallas_call(
        functools.partial(back_kernel, nt, nc, rows),
        out_shape=(
            jax.ShapeDtypeStruct((nt, rows, SLOT), BF16),
            jax.ShapeDtypeStruct((nt * rows, width), BF16),
        ),
        in_specs=[whole(pltpu.SMEM)] + [whole()] * 2,
        out_specs=(whole(), whole()),
        scratch_shapes=[pltpu.VMEM((SLOT, width), BF16)],
        compiler_params=PARAMS,
        cost_estimate=pl.CostEstimate(flops=flops, bytes_accessed=4 * nt * rows * width, transcendentals=0),
        name="hidden_grad_parts",
    )(odd_flag, grad_blocks, down_weight)
    forward = lax.all_to_all(forward, "row", 0, 0, tiled=True)
    back = lax.all_to_all(back, "row", 0, 0, tiled=True)
    packed = pl.pallas_call(
        functools.partial(swiglu_kernel, model, count),
        out_shape=jax.ShapeDtypeStruct((rows, 3 * SLOT), BF16),
        in_specs=[whole()] * 2,
        out_specs=whole(),
        compiler_params=PARAMS,
        cost_estimate=pl.CostEstimate(flops=20 * rows * SLOT, bytes_accessed=8 * rows * SLOT * nr, transcendentals=rows * SLOT),
        name="swiglu_grads",
    )(forward, back)
    packed = lax.all_gather(packed, "row", axis=0, tiled=True)

    chunk = 2 * feats
    blocks = pl.pallas_call(
        functools.partial(input_kernel, nt, rows, feats, count),
        out_shape=jax.ShapeDtypeStruct((nt, nc, rows + EXTRA, feats), BF16),
        grid=(width // chunk,),
        in_specs=[
            whole(),
            pl.BlockSpec((count, chunk), lambda j: (0, j)),
            pl.BlockSpec((count, chunk), lambda j: (0, j)),
            pl.BlockSpec((nt * rows, chunk), lambda j: (0, j)),
        ],
        out_specs=pl.BlockSpec((nt, 2, rows + EXTRA, feats), lambda j: (0, j, 0, 0)),
        scratch_shapes=[pltpu.VMEM((nt * rows, 1), F32), pltpu.VMEM((nt, EXTRA, 128), F32)],
        compiler_params=PARAMS,
        cost_estimate=pl.CostEstimate(flops=2 * flops, bytes_accessed=6 * nt * rows * width, transcendentals=0),
        name="input_grad_blocks",
    )(packed, gate_weight, up_weight, tokens_all)
    blocks = lax.all_to_all(blocks.reshape(nt * nc, rows + EXTRA, feats), ("tok", "col"), 0, 0, tiled=True)

    terms = jnp.einsum(
        "btf,btd->bfd",
        packed[:, :count].reshape(nt, rows, count),
        grad_all.reshape(nt, rows, width),
        preferred_element_type=F32,
    )
    terms = lax.optimization_barrier(terms.astype(BF16))
    d_down = jnp.sum(terms.astype(F32), axis=0).astype(BF16)

    own = lax.dynamic_slice_in_dim(packed, lax.axis_index("tok") * rows, rows)
    inv_own = own[:, count + 2 : count + 3].astype(F32) + own[:, count + 3 : count + 4].astype(F32)
    total = jnp.sum(blocks.astype(F32), axis=0)
    normed_grad = total[:rows]
    inner = (total[rows, :rows] + total[rows + 1, :rows]) / model
    d_gain = total[rows + 2] + total[rows + 3]
    scaled = tokens.astype(F32) * inv_own
    weighted = normed_grad * gain.astype(F32)
    d_tokens = (d_out.astype(F32) + inv_own * (weighted - scaled * inner[:, None])).astype(BF16)
    return (d_tokens, d_gain, d_down)


def solution(mesh):
    placed = (
        P("tok", ("row", "col")),
        P("tok", ("row", "col")),
        P(("row", "col")),
        P(("tok", "col"), "row"),
        P(("tok", "col"), "row"),
        P(("tok", "col"), "row"),
    )
    return jax.shard_map(
        on_device,
        mesh=mesh,
        in_specs=placed,
        out_specs=(P("tok", ("row", "col")), P(("row", "col")), P(("tok", "col"), "row")),
        check_vma=False,
    )
```

```python
import functools

import jax
import jax.numpy as jnp
from jax import lax
from jax.experimental import pallas as pl
from jax.experimental.pallas import tpu as pltpu
from jax.sharding import PartitionSpec as P

epsilon = 1e-05
F32 = jnp.float32
BF16 = jnp.bfloat16
AXES = ("tok", "row", "col")
SLOT = 256
EXTRA = 8
EXTRA_SENT = 16
NT_DIMS = (((1,), (1,)), ((), ()))
SMALL = pltpu.CompilerParams(vmem_limit_bytes=12 * 1024 * 1024)
LARGE = pltpu.CompilerParams(vmem_limit_bytes=24 * 1024 * 1024)


def split_wide(value):
    high = value.astype(BF16).astype(F32)
    return high, value - high


def mixed_groups(tok_count, row_count, col_count, even_along_tok):
    groups = []
    for row in range(row_count):
        if (row % 2 == 0) == even_along_tok:
            for col in range(col_count):
                groups.append([(tok * row_count + row) * col_count + col for tok in range(tok_count)])
        else:
            for tok in range(tok_count):
                groups.append([(tok * row_count + row) * col_count + col for col in range(col_count)])
    return groups


def weight_kernel(after_ref, gate_ref, up_ref, down_ref, out_ref):
    for place, weight in enumerate((gate_ref, up_ref, down_ref)):
        count, width = weight.shape
        out_ref[place, :count, :] = weight[...]
        out_ref[place, count:, :] = jnp.zeros((SLOT - count, width), BF16)


def forward_kernel(
    nt, nc, rows, count, odd_ref, blocks_ref, first_ref, w_ref, part_ref, tokens_ref, grads_ref, scaled_ref
):
    odd = odd_ref[0] == 1
    feats = blocks_ref.shape[2]
    gains = []
    for col in range(nc):
        late = blocks_ref[col, nt * 2 * rows :, :].astype(F32)
        early = first_ref[col, 2 * rows :, :].astype(F32)
        gains.append(jnp.where(odd, late, early)[0:1])
    totals = []
    for pair in range(nt // 2):
        at = pl.ds(pair * 2 * rows, 2 * rows)
        squares = jnp.zeros((2 * rows, feats), F32)
        for col in range(nc):
            two = []
            for tok in (2 * pair, 2 * pair + 1):
                outer, step = jnp.where(odd, col, tok), jnp.where(odd, tok, col)
                start = pl.multiple_of(step * (2 * rows), 16)
                two.append(blocks_ref[outer, pl.ds(start, 2 * rows), :].astype(F32))
            wide = jnp.concatenate([two[0][:rows], two[1][:rows]], axis=0)
            grads = jnp.concatenate([two[0][rows:], two[1][rows:]], axis=0)
            cols = pl.ds(col * feats, feats)
            tokens_ref[at, cols] = wide.astype(BF16)
            grads_ref[at, cols] = grads.astype(BF16)
            scaled_ref[at, cols] = (wide * gains[col]).astype(BF16)
            squares = squares + wide * wide
        totals.append(jnp.sum(squares, axis=1, keepdims=True))
    high, low = split_wide(jnp.concatenate(totals, axis=0))
    for place, source in enumerate((scaled_ref, scaled_ref, grads_ref)):
        value = lax.dot_general(source[...], w_ref[place], NT_DIMS, preferred_element_type=F32)
        if place == 0:
            lane = lax.broadcasted_iota(jnp.int32, value.shape, 1)
            value = jnp.where(lane == count, high, jnp.where(lane == count + 1, low, value))
        cols = pl.ds(place * SLOT, SLOT)
        for tok in range(nt):
            part_ref[tok, :, cols] = value[tok * rows : (tok + 1) * rows].astype(BF16)


def swiglu_kernel(model, count, parts_ref, packed_ref):
    sums = jnp.sum(parts_ref[...].astype(F32), axis=0)
    gate, up_proj, hidden_grad = sums[:, :SLOT], sums[:, SLOT : 2 * SLOT], sums[:, 2 * SLOT :]
    lane = lax.broadcasted_iota(jnp.int32, gate.shape, 1)
    at_squares = (lane >= count) & (lane < count + 2)
    squares = jnp.sum(jnp.where(at_squares, gate, 0.0), axis=1, keepdims=True)
    inv_rms = lax.rsqrt(squares / model + epsilon)
    gate = jnp.where(lane < count, gate * inv_rms, 0.0)
    up_proj = up_proj * inv_rms
    sig = jax.nn.sigmoid(gate)
    hidden = gate * sig * up_proj
    gate_grad = (hidden_grad * up_proj * sig * (1.0 + gate * (1.0 - sig))).astype(BF16)
    up_grad = (hidden_grad * gate * sig).astype(BF16)
    inner = jnp.sum(gate_grad.astype(F32) * gate + up_grad.astype(F32) * up_proj, axis=1, keepdims=True)
    for place, value in enumerate(split_wide(inner) + split_wide(inv_rms)):
        hidden = jnp.where(lane == count + place, value, hidden)
    packed_ref[:, :SLOT] = hidden.astype(BF16)
    packed_ref[:, SLOT : 2 * SLOT] = gate_grad
    packed_ref[:, 2 * SLOT :] = up_grad


def input_kernel(nt, rows, feats, count, packed_ref, gate_ref, up_ref, tokens_ref, out_ref, inv_ref, extra_ref):
    base = count % 128

    @pl.when(pl.program_id(0) == 0)
    def _():
        tail = packed_ref[:, SLOT - 128 : SLOT].astype(F32)
        lane = lax.broadcasted_iota(jnp.int32, tail.shape, 1)
        at_inv = (lane >= base + 2) & (lane < base + 4)
        inv_ref[...] = jnp.sum(jnp.where(at_inv, tail, 0.0), axis=1, keepdims=True)
        for tok in range(nt):
            piece = tail[tok * rows : (tok + 1) * rows]
            square = jnp.concatenate([piece, jnp.zeros((128 - rows, 128), F32)], axis=0)
            extra_ref[tok] = square.T[base : base + EXTRA]

    term = jnp.dot(packed_ref[:, SLOT : 2 * SLOT], gate_ref[0], preferred_element_type=F32)
    term = term + jnp.dot(packed_ref[:, 2 * SLOT :], up_ref[0], preferred_element_type=F32)
    gain_term = jnp.sum(term * (tokens_ref[...].astype(F32) * inv_ref[...]), axis=0, keepdims=True)
    high, low = split_wide(gain_term)
    spot = lax.broadcasted_iota(jnp.int32, (EXTRA, feats), 0)
    for part in range(gate_ref.shape[2] // feats):
        cols = slice(part * feats, (part + 1) * feats)
        for tok in range(nt):
            extra = jnp.where(spot == 2, high[:, cols], jnp.where(spot == 3, low[:, cols], extra_ref[tok]))
            block = jnp.concatenate([term[tok * rows : (tok + 1) * rows, cols], extra], axis=0)
            out_ref[tok, part] = block.astype(BF16)


def copy_kernel(copies, own_ref, out_ref):
    own = own_ref[...].astype(F32)
    gain = jnp.broadcast_to(own[-1:], (EXTRA_SENT, own.shape[1]))
    block = jnp.concatenate([own[:-1], gain], axis=0).astype(BF16)
    for copy in range(copies):
        out_ref[copy] = block


def message_kernel(rows, first_ref, out_ref):
    count = first_ref.shape[0]
    for at in range(count):
        out_ref[pl.ds(at * rows, rows), :] = first_ref[at, :rows, :]
    out_ref[count * rows :, :] = first_ref[0, rows:, :]


def final_kernel(model, blocks_ref, tokens_ref, grads_ref, gain_ref, inv_ref, tokens_out_ref, gain_out_ref):
    rows, feats = tokens_ref.shape
    total = lax.fori_loop(
        1,
        blocks_ref.shape[0],
        lambda at, running: running + blocks_ref[at].astype(F32),
        blocks_ref[0].astype(F32),
        unroll=7,
    )
    extra = total[rows:]
    turned = jnp.concatenate([extra, jnp.zeros((feats - EXTRA, feats), F32)], axis=0).T
    inner = (turned[:rows, 0:1] + turned[:rows, 1:2]) / model
    gain_out_ref[...] = extra[2:3] + extra[3:4]
    inv = inv_ref[...]
    scaled = tokens_ref[...].astype(F32) * inv
    weighted = total[:rows] * gain_ref[...].astype(F32)
    result = grads_ref[...].astype(F32) + inv * (weighted - scaled * inner)
    tokens_out_ref[...] = result.astype(BF16)


def whole(memory=pltpu.VMEM):
    return pl.BlockSpec(memory_space=memory)


def on_device(tokens, d_out, gain, gate_weight, up_weight, down_weight):
    nt, nr, nc = (lax.axis_size(a) for a in AXES)
    rows, feats = tokens.shape
    count = gate_weight.shape[0]
    width = nc * feats
    model = nr * width
    odd = lax.rem(lax.axis_index("row"), 2)
    odd_flag = odd.reshape(1).astype(jnp.int32)

    gain_row = gain.reshape(1, feats)
    tall = 2 * rows + EXTRA_SENT
    copies = pl.pallas_call(
        functools.partial(copy_kernel, nc),
        out_shape=jax.ShapeDtypeStruct((nc, tall, feats), BF16),
        in_specs=[whole()],
        out_specs=whole(),
        compiler_params=SMALL,
        name="own_copies",
    )(jnp.concatenate([tokens, d_out, gain_row], axis=0))
    first = mixed_groups(nt, nr, nc, False)
    stage = lax.all_to_all(copies, AXES, 0, 0, tiled=True, axis_index_groups=first)
    long = nc * 2 * rows + EXTRA_SENT
    message = pl.pallas_call(
        functools.partial(message_kernel, 2 * rows),
        out_shape=jax.ShapeDtypeStruct((long, feats), BF16),
        in_specs=[whole()],
        out_specs=whole(),
        compiler_params=SMALL,
        name="second_message",
    )(stage)
    copies = jnp.broadcast_to(message[None], (nt, long, feats))
    second = mixed_groups(nt, nr, nc, True)
    both = lax.all_to_all(copies, AXES, 0, 0, tiled=True, axis_index_groups=second)

    flops = 2 * nt * rows * width * SLOT
    weights = pl.pallas_call(
        weight_kernel,
        out_shape=jax.ShapeDtypeStruct((3, SLOT, width), BF16),
        grid=(1,),
        in_specs=[pl.BlockSpec((1, 16, feats), lambda j: (0, 0, 0))]
        + [pl.BlockSpec((count, width), lambda j: (0, 0))] * 3,
        out_specs=pl.BlockSpec((3, SLOT, width), lambda j: (0, 0, 0)),
        compiler_params=SMALL,
        cost_estimate=pl.CostEstimate(flops=0, bytes_accessed=12 * SLOT * width, transcendentals=0),
        name="padded_weights",
    )(stage, gate_weight, up_weight, down_weight)
    parts, tokens_all, grad_all = pl.pallas_call(
        functools.partial(forward_kernel, nt, nc, rows, count),
        out_shape=(
            jax.ShapeDtypeStruct((nt, rows, 3 * SLOT), BF16),
            jax.ShapeDtypeStruct((nt * rows, width), BF16),
            jax.ShapeDtypeStruct((nt * rows, width), BF16),
        ),
        in_specs=[whole(pltpu.SMEM)] + [whole()] * 3,
        out_specs=(whole(), whole(), whole()),
        scratch_shapes=[pltpu.VMEM((nt * rows, width), BF16)],
        compiler_params=LARGE,
        cost_estimate=pl.CostEstimate(flops=3 * flops, bytes_accessed=8 * nt * rows * width, transcendentals=0),
        name="forward_parts",
    )(odd_flag, both, stage, weights)
    parts = lax.all_to_all(parts, "row", 0, 0, tiled=True)
    packed = pl.pallas_call(
        functools.partial(swiglu_kernel, model, count),
        out_shape=jax.ShapeDtypeStruct((rows, 3 * SLOT), BF16),
        in_specs=[whole()],
        out_specs=whole(),
        compiler_params=SMALL,
        cost_estimate=pl.CostEstimate(flops=20 * rows * SLOT, bytes_accessed=8 * rows * SLOT * nr, transcendentals=rows * SLOT),
        name="swiglu_grads",
    )(parts)
    packed = lax.all_gather(packed, "row", axis=0, tiled=True)

    chunk = 2 * feats
    blocks = pl.pallas_call(
        functools.partial(input_kernel, nt, rows, feats, count),
        out_shape=jax.ShapeDtypeStruct((nt, nc, rows + EXTRA, feats), BF16),
        grid=(width // chunk,),
        in_specs=[
            whole(),
            pl.BlockSpec((1, SLOT, chunk), lambda j: (0, 0, j)),
            pl.BlockSpec((1, SLOT, chunk), lambda j: (1, 0, j)),
            pl.BlockSpec((nt * rows, chunk), lambda j: (0, j)),
        ],
        out_specs=pl.BlockSpec((nt, 2, rows + EXTRA, feats), lambda j: (0, j, 0, 0)),
        scratch_shapes=[pltpu.VMEM((nt * rows, 1), F32), pltpu.VMEM((nt, EXTRA, 128), F32)],
        compiler_params=LARGE,
        cost_estimate=pl.CostEstimate(flops=2 * flops, bytes_accessed=6 * nt * rows * width, transcendentals=0),
        name="input_grad_blocks",
    )(packed, weights, weights, tokens_all)
    blocks = lax.all_to_all(blocks.reshape(nt * nc, rows + EXTRA, feats), ("tok", "col"), 0, 0, tiled=True)

    terms = jnp.einsum(
        "btf,btd->bfd",
        packed[:, :count].reshape(nt, rows, count),
        grad_all.reshape(nt, rows, width),
        preferred_element_type=F32,
    )
    terms = lax.optimization_barrier(terms.astype(BF16))
    d_down = jnp.sum(terms.astype(F32), axis=0).astype(BF16)

    own = lax.dynamic_slice_in_dim(packed, lax.axis_index("tok") * rows, rows)
    inv_own = own[:, count + 2 : count + 3].astype(F32) + own[:, count + 3 : count + 4].astype(F32)
    d_tokens, d_gain = pl.pallas_call(
        functools.partial(final_kernel, model),
        out_shape=(
            jax.ShapeDtypeStruct((rows, feats), BF16),
            jax.ShapeDtypeStruct((1, feats), F32),
        ),
        in_specs=[whole()] * 5,
        out_specs=(whole(), whole()),
        compiler_params=SMALL,
        name="token_grads",
    )(blocks, tokens, d_out, gain_row, inv_own)
    d_gain = d_gain.reshape(feats)
    return (d_tokens, d_gain, d_down)


def solution(mesh):
    placed = (
        P("tok", ("row", "col")),
        P("tok", ("row", "col")),
        P(("row", "col")),
        P(("tok", "col"), "row"),
        P(("tok", "col"), "row"),
        P(("tok", "col"), "row"),
    )
    return jax.shard_map(
        on_device,
        mesh=mesh,
        in_specs=placed,
        out_specs=(P("tok", ("row", "col")), P(("row", "col")), P(("tok", "col"), "row")),
        check_vma=False,
    )
```

```python
import functools

import jax
import jax.numpy as jnp
from jax import lax
from jax.experimental import pallas as pl
from jax.experimental.pallas import tpu as pltpu
from jax.sharding import PartitionSpec as P

epsilon = 1e-05
F32 = jnp.float32
BF16 = jnp.bfloat16
AXES = ("tok", "row", "col")
SLOT = 256
EXTRA = 8
EXTRA_SENT = 16
WINDOW = 40
SHIFT = 32
TN_DIMS = (((0,), (0,)), ((), ()))
NT_DIMS = (((1,), (1,)), ((), ()))
SMALL = pltpu.CompilerParams(vmem_limit_bytes=12 * 1024 * 1024)
WIDE = pltpu.CompilerParams(vmem_limit_bytes=59 * 1024 * 1024)
LARGE = pltpu.CompilerParams(vmem_limit_bytes=24 * 1024 * 1024)


def split_wide(value):
    high = value.astype(BF16).astype(F32)
    return high, value - high


def mixed_groups(tok_count, row_count, col_count, even_along_tok):
    groups = []
    for row in range(row_count):
        if (row % 2 == 0) == even_along_tok:
            for col in range(col_count):
                groups.append([(tok * row_count + row) * col_count + col for tok in range(tok_count)])
        else:
            for tok in range(tok_count):
                groups.append([(tok * row_count + row) * col_count + col for col in range(col_count)])
    return groups


def weight_kernel(after_ref, gate_ref, up_ref, down_ref, out_ref, sent_ref):
    for place, weight in enumerate((gate_ref, up_ref, down_ref)):
        count, width = weight.shape
        out_ref[place, :count, :] = weight[...]
        out_ref[place, count:, :] = jnp.zeros((SLOT - count, width), BF16)
        if place < 2:
            sent_ref[place] = weight[...]


def valid_rows(shape, side):
    row = lax.broadcasted_iota(jnp.int32, shape, 0)
    return (row >= 4 * side) & (row < WINDOW - 4 + 4 * side)


def join_windows(low, high):
    row = lax.broadcasted_iota(jnp.int32, (8,) + low.shape[1:], 0)
    shared = jnp.where(row < 4, low[SHIFT:], high[: WINDOW - SHIFT])
    return jnp.concatenate([low[:SHIFT], shared, high[WINDOW - SHIFT :]], axis=0)


def block_pair(blocks_ref, odd, pair, col, rows):
    two = []
    for tok in (2 * pair, 2 * pair + 1):
        outer, step = jnp.where(odd, col, tok), jnp.where(odd, tok, col)
        start = pl.multiple_of(step * (2 * rows), 16)
        two.append(blocks_ref[outer, pl.ds(start, 2 * rows), :].astype(F32))
    return two


def forward_kernel(
    nt, nc, rows, count, flag_ref, blocks_ref, first_ref, w_ref, part_ref, grads_ref, scaled_ref
):
    odd = flag_ref[0] == 1
    feats = blocks_ref.shape[2]
    gains = []
    for col in range(nc):
        late = blocks_ref[col, nt * 2 * rows :, :].astype(F32)
        early = first_ref[col, 2 * rows :, :].astype(F32)
        gains.append(jnp.where(odd, late, early)[0:1])
    totals = []
    for pair in range(nt // 2):
        at = pl.ds(pair * 2 * rows, 2 * rows)
        squares = jnp.zeros((2 * rows, feats), F32)
        for col in range(nc):
            two = block_pair(blocks_ref, odd, pair, col, rows)
            wide = jnp.concatenate([two[0][:rows], two[1][:rows]], axis=0)
            grads = jnp.concatenate([two[0][rows:], two[1][rows:]], axis=0)
            cols = pl.ds(col * feats, feats)
            grads_ref[at, cols] = grads.astype(BF16)
            scaled_ref[at, cols] = (wide * gains[col]).astype(BF16)
            squares = squares + wide * wide
        totals.append(jnp.sum(squares, axis=1, keepdims=True))
    high, low = split_wide(jnp.concatenate(totals, axis=0))
    for place, source in enumerate((scaled_ref, scaled_ref, grads_ref)):
        value = lax.dot_general(source[...], w_ref[place], NT_DIMS, preferred_element_type=F32)
        if place == 0:
            lane = lax.broadcasted_iota(jnp.int32, value.shape, 1)
            value = jnp.where(lane == count, high, jnp.where(lane == count + 1, low, value))
        cols = pl.ds(place * SLOT, SLOT)
        for tok in range(nt):
            for half in range(2):
                start = tok * rows + half * SHIFT
                part_ref[2 * tok + half, :, cols] = value[start : start + WINDOW].astype(BF16)


def windows_kernel(nt, nc, rows, flag_ref, blocks_ref, after_ref, tokens_ref, grads_ref):
    odd = flag_ref[0] == 1
    side = flag_ref[1] == 1
    feats = blocks_ref.shape[2]
    for pair in range(nt // 2):
        at = pl.ds(pair * 2 * WINDOW, 2 * WINDOW)
        for col in range(nc):
            two = block_pair(blocks_ref, odd, pair, col, rows)
            cols = pl.ds(col * feats, feats)
            low, high = [], []
            for start in (0, rows):
                low.append(jnp.concatenate([half[start : start + WINDOW] for half in two], axis=0))
                late = start + SHIFT
                high.append(jnp.concatenate([half[late : late + WINDOW] for half in two], axis=0))
            tokens_ref[at, cols] = jnp.where(side, high[0], low[0]).astype(BF16)
            grads_ref[0, at, cols] = jnp.where(side, high[1], low[1]).astype(BF16)
            grads_ref[1, at, cols] = jnp.where(side, low[1], high[1]).astype(BF16)


def swiglu_kernel(model, count, flag_ref, parts_ref, packed_ref):
    side = flag_ref[1]
    members = parts_ref.shape[0] // 2

    def summed(parity):
        total = parts_ref[parity].astype(F32)
        for at in range(1, members):
            total = total + parts_ref[2 * at + parity].astype(F32)
        return total

    inner = jnp.zeros((WINDOW, 1), F32)
    inv_rms = None
    for place, parity in enumerate((side, 1 - side)):
        sums = summed(parity)
        gate, up_proj, hidden_grad = sums[:, :SLOT], sums[:, SLOT : 2 * SLOT], sums[:, 2 * SLOT :]
        lane = lax.broadcasted_iota(jnp.int32, gate.shape, 1)
        if place == 0:
            at_squares = (lane >= count) & (lane < count + 2)
            squares = jnp.sum(jnp.where(at_squares, gate, 0.0), axis=1, keepdims=True)
            inv_rms = lax.rsqrt(squares / model + epsilon)
        keep = valid_rows(gate.shape, side) & (lane < count)
        gate = jnp.where(keep, gate * inv_rms, 0.0)
        up_proj = up_proj * inv_rms
        sig = jax.nn.sigmoid(gate)
        hidden = jnp.where(keep, gate * sig * up_proj, 0.0)
        gate_grad = jnp.where(keep, hidden_grad * up_proj * sig * (1.0 + gate * (1.0 - sig)), 0.0)
        up_grad = jnp.where(keep, hidden_grad * gate * sig, 0.0)
        gate_grad, up_grad = gate_grad.astype(BF16), up_grad.astype(BF16)
        inner_term = gate_grad.astype(F32) * gate + up_grad.astype(F32) * up_proj
        inner = inner + jnp.sum(inner_term, axis=1, keepdims=True)
        packed_ref[:, (2 * place) * SLOT : (2 * place + 1) * SLOT] = gate_grad
        packed_ref[:, (2 * place + 1) * SLOT : (2 * place + 2) * SLOT] = up_grad
        packed_ref[:, (4 + place) * SLOT : (5 + place) * SLOT] = hidden.astype(BF16)
    own = packed_ref[:, :SLOT].astype(F32)
    lane = lax.broadcasted_iota(jnp.int32, own.shape, 1)
    for place, value in enumerate((split_wide(inner) + split_wide(inv_rms)) * 2):
        own = jnp.where(lane == count + place, value, own)
    packed_ref[:, :SLOT] = own.astype(BF16)


def input_kernel(
    nt,
    shares,
    feats,
    count,
    flag_ref,
    packed_ref,
    own_ref,
    other_ref,
    tokens_ref,
    out_ref,
    inv_ref,
    extra_ref,
):
    base = count % 128
    side = flag_ref[1]
    spot = lax.broadcasted_iota(jnp.int32, (EXTRA, feats), 0) % 4

    @pl.when(pl.program_id(0) == 0)
    def _():
        tail = packed_ref[:, SLOT - 128 : SLOT].astype(F32)
        lane = lax.broadcasted_iota(jnp.int32, tail.shape, 1)
        at_inv = (lane >= base + 2) & (lane < base + 4)
        inv_ref[...] = jnp.sum(jnp.where(at_inv, tail, 0.0), axis=1, keepdims=True)
        for tok in range(nt):
            piece = tail[tok * WINDOW : (tok + 1) * WINDOW]
            square = jnp.concatenate([piece, jnp.zeros((128 - WINDOW, 128), F32)], axis=0)
            turned = square.T[base : base + EXTRA]
            share = jnp.where(flag_ref[2] == 1, turned[3:4], turned[2:3]) * (1.0 / shares)
            extra_ref[tok] = jnp.where(spot == 3, share, turned)

    fill = jnp.zeros((SLOT - count, own_ref.shape[2]), BF16)
    weights = [own_ref[0], own_ref[1]]
    weights += [jnp.concatenate([other_ref[place], fill], axis=0) for place in range(2)]
    term = jnp.zeros((packed_ref.shape[0], own_ref.shape[2]), F32)
    for place, weight in enumerate(weights):
        values = packed_ref[:, place * SLOT : (place + 1) * SLOT]
        term = term + jnp.dot(values, weight, preferred_element_type=F32)
    gain_term = jnp.sum(term * (tokens_ref[...].astype(F32) * inv_ref[...]), axis=0, keepdims=True)
    keep = valid_rows((WINDOW, feats), side)
    for part in range(own_ref.shape[2] // feats):
        cols = slice(part * feats, (part + 1) * feats)
        for tok in range(nt):
            extra = jnp.where(spot == 2, gain_term[:, cols], extra_ref[tok])
            extra = jnp.concatenate([extra] * (WINDOW // EXTRA), axis=0)
            block = jnp.where(keep, term[tok * WINDOW : (tok + 1) * WINDOW, cols], extra)
            out_ref[tok, part] = block.astype(BF16)


def down_mine_kernel(hidden_ref, grads_ref, out_ref):
    out_ref[...] = lax.dot_general(hidden_ref[...], grads_ref[0], TN_DIMS, preferred_element_type=F32)


def down_other_kernel(hidden_ref, grads_ref, mine_ref, out_ref):
    total = lax.dot_general(hidden_ref[...], grads_ref[0], TN_DIMS, preferred_element_type=F32)
    out_ref[...] = (total + mine_ref[...])[: out_ref.shape[0]].astype(BF16)


def copy_kernel(copies, own_ref, out_ref):
    own = own_ref[...].astype(F32)
    gain = jnp.broadcast_to(own[-1:], (EXTRA_SENT, own.shape[1]))
    block = jnp.concatenate([own[:-1], gain], axis=0).astype(BF16)
    for copy in range(copies):
        out_ref[copy] = block


def message_kernel(rows, first_ref, out_ref):
    count = first_ref.shape[0]
    for at in range(count):
        out_ref[pl.ds(at * rows, rows), :] = first_ref[at, :rows, :]
    out_ref[count * rows :, :] = first_ref[0, rows:, :]


def final_kernel(model, blocks_ref, tokens_ref, grads_ref, gain_ref, tokens_out_ref, gain_out_ref):
    rows, feats = tokens_ref.shape

    def add(at, sums):
        return (
            sums[0] + blocks_ref[2 * at].astype(F32),
            sums[1] + blocks_ref[2 * at + 1].astype(F32),
        )

    start = (blocks_ref[0].astype(F32), blocks_ref[1].astype(F32))
    low, high = lax.fori_loop(1, blocks_ref.shape[0] // 2, add, start)
    rest = jnp.zeros((feats - EXTRA, feats), F32)
    low_turned = jnp.concatenate([low[SHIFT:], rest], axis=0).T[:WINDOW]
    high_turned = jnp.concatenate([high[:EXTRA], rest], axis=0).T[:WINDOW]
    inner = join_windows(low_turned[:, 4:5] + low_turned[:, 5:6], high_turned[:, 0:1] + high_turned[:, 1:2])
    inner = inner / model
    inv = join_windows(low_turned[:, 7:8], high_turned[:, 3:4])
    gain_out_ref[...] = low[SHIFT + 6 : SHIFT + 7] + high[2:3]
    scaled = tokens_ref[...].astype(F32) * inv
    weighted = join_windows(low, high) * gain_ref[...].astype(F32)
    result = grads_ref[...].astype(F32) + inv * (weighted - scaled * inner)
    tokens_out_ref[...] = result.astype(BF16)


def whole(memory=pltpu.VMEM):
    return pl.BlockSpec(memory_space=memory)


def on_device(tokens, d_out, gain, gate_weight, up_weight, down_weight):
    nt, nr, nc = (lax.axis_size(a) for a in AXES)
    rows, feats = tokens.shape
    count = gate_weight.shape[0]
    width = nc * feats
    model = nr * width
    flags = jnp.stack([lax.rem(lax.axis_index(a), 2) for a in ("row", "col", "tok")]).astype(jnp.int32)

    neighbours = [(at, at ^ 1) for at in range(nc)]
    gain_row = gain.reshape(1, feats)
    tall = 2 * rows + EXTRA_SENT
    copies = pl.pallas_call(
        functools.partial(copy_kernel, nc),
        out_shape=jax.ShapeDtypeStruct((nc, tall, feats), BF16),
        in_specs=[whole()],
        out_specs=whole(),
        compiler_params=SMALL,
        name="own_copies",
    )(jnp.concatenate([tokens, d_out, gain_row], axis=0))
    first = mixed_groups(nt, nr, nc, False)
    stage = lax.all_to_all(copies, AXES, 0, 0, tiled=True, axis_index_groups=first)
    long = nc * 2 * rows + EXTRA_SENT
    message = pl.pallas_call(
        functools.partial(message_kernel, 2 * rows),
        out_shape=jax.ShapeDtypeStruct((long, feats), BF16),
        in_specs=[whole()],
        out_specs=whole(),
        compiler_params=SMALL,
        name="second_message",
    )(stage)
    copies = jnp.broadcast_to(message[None], (nt, long, feats))
    second = mixed_groups(nt, nr, nc, True)
    both = lax.all_to_all(copies, AXES, 0, 0, tiled=True, axis_index_groups=second)

    flops = 2 * nt * rows * width * SLOT
    weights, sent = pl.pallas_call(
        weight_kernel,
        out_shape=(
            jax.ShapeDtypeStruct((3, SLOT, width), BF16),
            jax.ShapeDtypeStruct((2, count, width), BF16),
        ),
        in_specs=[whole(pl.ANY)] + [whole()] * 3,
        out_specs=(whole(), whole()),
        compiler_params=SMALL,
        cost_estimate=pl.CostEstimate(flops=0, bytes_accessed=12 * SLOT * width, transcendentals=0),
        name="padded_weights",
    )(stage, gate_weight, up_weight, down_weight)
    parts = pl.pallas_call(
        functools.partial(forward_kernel, nt, nc, rows, count),
        out_shape=jax.ShapeDtypeStruct((2 * nt, WINDOW, 3 * SLOT), BF16),
        in_specs=[whole(pltpu.SMEM)] + [whole()] * 3,
        out_specs=whole(),
        scratch_shapes=[pltpu.VMEM((nt * rows, width), BF16)] * 2,
        compiler_params=LARGE,
        cost_estimate=pl.CostEstimate(flops=3 * flops, bytes_accessed=8 * nt * rows * width, transcendentals=0),
        name="forward_parts",
    )(flags, both, stage, weights)
    tokens_all, grad_all = pl.pallas_call(
        functools.partial(windows_kernel, nt, nc, rows),
        out_shape=(
            jax.ShapeDtypeStruct((nt * WINDOW, width), BF16),
            jax.ShapeDtypeStruct((2, nt * WINDOW, width), BF16),
        ),
        in_specs=[whole(pltpu.SMEM), whole(), whole(pl.ANY)],
        out_specs=(whole(), whole()),
        compiler_params=LARGE,
        cost_estimate=pl.CostEstimate(flops=0, bytes_accessed=8 * nt * rows * width, transcendentals=0),
        name="token_windows",
    )(flags, both, parts)
    sent, parts = lax.optimization_barrier((sent, parts))
    sent = lax.ppermute(sent, "col", neighbours)
    pairs = [
        [(tok * nr + row) * nc + 2 * pair + side for row in range(nr) for side in range(2)]
        for tok in range(nt)
        for pair in range(nc // 2)
    ]
    parts = lax.all_to_all(parts, AXES, 0, 0, tiled=True, axis_index_groups=pairs)
    packed = pl.pallas_call(
        functools.partial(swiglu_kernel, model, count),
        out_shape=jax.ShapeDtypeStruct((WINDOW, 6 * SLOT), BF16),
        in_specs=[whole(pltpu.SMEM), whole()],
        out_specs=whole(),
        compiler_params=SMALL,
        cost_estimate=pl.CostEstimate(
            flops=40 * WINDOW * SLOT, bytes_accessed=16 * WINDOW * SLOT * nr, transcendentals=2 * WINDOW * SLOT
        ),
        name="swiglu_grads",
    )(flags, parts)
    packed = lax.all_gather(packed, "row", axis=0, tiled=True)

    chunk = 2 * feats
    blocks = pl.pallas_call(
        functools.partial(input_kernel, nt, nt * nc // 4, feats, count),
        out_shape=jax.ShapeDtypeStruct((nt, nc, WINDOW, feats), BF16),
        grid=(width // chunk,),
        in_specs=[
            whole(pltpu.SMEM),
            whole(),
            pl.BlockSpec((2, SLOT, chunk), lambda j: (0, 0, j)),
            pl.BlockSpec((2, count, chunk), lambda j: (0, 0, j)),
            pl.BlockSpec((nt * WINDOW, chunk), lambda j: (0, j)),
        ],
        out_specs=pl.BlockSpec((nt, 2, WINDOW, feats), lambda j: (0, j, 0, 0)),
        scratch_shapes=[pltpu.VMEM((nt * WINDOW, 1), F32), pltpu.VMEM((nt, EXTRA, 128), F32)],
        compiler_params=LARGE,
        cost_estimate=pl.CostEstimate(flops=2 * flops, bytes_accessed=6 * nt * rows * width, transcendentals=0),
        name="input_grad_blocks",
    )(flags, packed, weights, sent, tokens_all)
    blocks = lax.all_to_all(blocks.reshape(nt * nc, WINDOW, feats), ("tok", "col"), 0, 0, tiled=True)

    hidden_other = lax.ppermute(packed[:, 5 * SLOT :], "col", neighbours)
    half_chunk = width // 2
    down_cost = pl.CostEstimate(flops=flops // 2, bytes_accessed=3 * nt * rows * width, transcendentals=0)
    mine = pl.pallas_call(
        down_mine_kernel,
        out_shape=jax.ShapeDtypeStruct((SLOT, width), F32),
        grid=(2,),
        in_specs=[
            pl.BlockSpec((nt * WINDOW, SLOT), lambda j: (0, 4)),
            pl.BlockSpec((1, nt * WINDOW, half_chunk), lambda j: (0, 0, j)),
        ],
        out_specs=pl.BlockSpec((SLOT, half_chunk), lambda j: (0, j)),
        compiler_params=LARGE,
        cost_estimate=down_cost,
        name="down_grads_mine",
    )(packed, grad_all)
    d_down = pl.pallas_call(
        down_other_kernel,
        out_shape=jax.ShapeDtypeStruct((count, width), BF16),
        grid=(2,),
        in_specs=[
            pl.BlockSpec((nt * WINDOW, SLOT), lambda j: (0, 0)),
            pl.BlockSpec((1, nt * WINDOW, half_chunk), lambda j: (1, 0, j)),
            pl.BlockSpec((SLOT, half_chunk), lambda j: (0, j)),
        ],
        out_specs=pl.BlockSpec((count, half_chunk), lambda j: (0, j)),
        compiler_params=LARGE,
        cost_estimate=down_cost,
        name="down_grads",
    )(hidden_other, grad_all, mine)

    d_tokens, d_gain = pl.pallas_call(
        functools.partial(final_kernel, model),
        out_shape=(
            jax.ShapeDtypeStruct((rows, feats), BF16),
            jax.ShapeDtypeStruct((1, feats), F32),
        ),
        in_specs=[whole()] * 4,
        out_specs=(whole(), whole()),
        compiler_params=SMALL,
        name="token_grads",
    )(blocks, tokens, d_out, gain_row)
    d_gain = d_gain.reshape(feats)
    return (d_tokens, d_gain, d_down)


def solution(mesh):
    placed = (
        P("tok", ("row", "col")),
        P("tok", ("row", "col")),
        P(("row", "col")),
        P(("tok", "col"), "row"),
        P(("tok", "col"), "row"),
        P(("tok", "col"), "row"),
    )
    return jax.shard_map(
        on_device,
        mesh=mesh,
        in_specs=placed,
        out_specs=(P("tok", ("row", "col")), P(("row", "col")), P(("tok", "col"), "row")),
        check_vma=False,
    )
```

```python
import functools

import jax
import jax.numpy as jnp
from jax import lax
from jax.experimental import pallas as pl
from jax.experimental.pallas import tpu as pltpu
from jax.sharding import PartitionSpec as P

epsilon = 1e-05
F32 = jnp.float32
BF16 = jnp.bfloat16
AXES = ("tok", "row", "col")
SLOT = 256
EXTRA = 8
EXTRA_SENT = 16
WINDOW = 40
SHIFT = 32
TN_DIMS = (((0,), (0,)), ((), ()))
NT_DIMS = (((1,), (1,)), ((), ()))
SMALL = pltpu.CompilerParams(vmem_limit_bytes=12 * 1024 * 1024)
WIDE = pltpu.CompilerParams(vmem_limit_bytes=59 * 1024 * 1024)
LARGE = pltpu.CompilerParams(vmem_limit_bytes=24 * 1024 * 1024)


def axis_parity(axis):
    return lax.rem(lax.axis_index(axis), 2)


def split_wide(value):
    high = value.astype(BF16).astype(F32)
    return high, value - high


def mixed_groups(tok_count, row_count, col_count, even_along_tok):
    groups = []
    for row in range(row_count):
        if (row % 2 == 0) == even_along_tok:
            for col in range(col_count):
                groups.append([(tok * row_count + row) * col_count + col for tok in range(tok_count)])
        else:
            for tok in range(tok_count):
                groups.append([(tok * row_count + row) * col_count + col for col in range(col_count)])
    return groups


def padded_weight(ref, scratch):
    count = ref.shape[0]
    scratch[:count, :] = ref[...]
    scratch[count:, :] = jnp.zeros((scratch.shape[0] - count, ref.shape[1]), BF16)
    return scratch[...]


def valid_rows(shape, side):
    row = lax.broadcasted_iota(jnp.int32, shape, 0)
    return (row >= 4 * side) & (row < WINDOW - 4 + 4 * side)


def join_windows(low, high):
    row = lax.broadcasted_iota(jnp.int32, (8,) + low.shape[1:], 0)
    shared = jnp.where(row < 4, low[SHIFT:], high[: WINDOW - SHIFT])
    return jnp.concatenate([low[:SHIFT], shared, high[WINDOW - SHIFT :]], axis=0)


def block_pair(blocks_ref, odd, pair, col, rows):
    two = []
    for tok in (2 * pair, 2 * pair + 1):
        outer, step = jnp.where(odd, col, tok), jnp.where(odd, tok, col)
        start = pl.multiple_of(step * (2 * rows), 16)
        two.append(blocks_ref[outer, pl.ds(start, 2 * rows), :].astype(F32))
    return two


def forward_kernel(
    nt,
    nc,
    rows,
    count,
    blocks_ref,
    first_ref,
    gate_ref,
    up_ref,
    down_ref,
    part_ref,
    grads_ref,
    scaled_ref,
    w_ref,
):
    odd = axis_parity("row") == 1
    feats = blocks_ref.shape[2]
    gains = []
    for col in range(nc):
        late = blocks_ref[col, nt * 2 * rows :, :].astype(F32)
        early = first_ref[col, 2 * rows :, :].astype(F32)
        gains.append(jnp.where(odd, late, early)[0:1])
    totals = []
    for pair in range(nt // 2):
        at = pl.ds(pair * 2 * rows, 2 * rows)
        squares = jnp.zeros((2 * rows, feats), F32)
        for col in range(nc):
            two = block_pair(blocks_ref, odd, pair, col, rows)
            wide = jnp.concatenate([two[0][:rows], two[1][:rows]], axis=0)
            grads = jnp.concatenate([two[0][rows:], two[1][rows:]], axis=0)
            cols = pl.ds(col * feats, feats)
            grads_ref[at, cols] = grads.astype(BF16)
            scaled_ref[at, cols] = (wide * gains[col]).astype(BF16)
            squares = squares + wide * wide
        totals.append(jnp.sum(squares, axis=1, keepdims=True))
    high, low = split_wide(jnp.concatenate(totals, axis=0))
    for place, (source, weight) in enumerate(((scaled_ref, gate_ref), (scaled_ref, up_ref), (grads_ref, down_ref))):
        padded = padded_weight(weight, w_ref.at[place])
        value = lax.dot_general(source[...], padded, NT_DIMS, preferred_element_type=F32)
        if place == 0:
            lane = lax.broadcasted_iota(jnp.int32, value.shape, 1)
            value = jnp.where(lane == count, high, jnp.where(lane == count + 1, low, value))
        cols = pl.ds(place * SLOT, SLOT)
        for tok in range(nt):
            for half in range(2):
                start = tok * rows + half * SHIFT
                part_ref[2 * tok + half, :, cols] = value[start : start + WINDOW].astype(BF16)


def windows_kernel(nt, nc, rows, blocks_ref, after_ref, tokens_ref, mine_ref, other_ref):
    odd = axis_parity("row") == 1
    side = axis_parity("col") == 1
    feats = blocks_ref.shape[2]
    for pair in range(nt // 2):
        at = pl.ds(pair * 2 * WINDOW, 2 * WINDOW)
        for col in range(nc):
            two = block_pair(blocks_ref, odd, pair, col, rows)
            cols = pl.ds(col * feats, feats)
            low, high = [], []
            for start in (0, rows):
                low.append(jnp.concatenate([half[start : start + WINDOW] for half in two], axis=0))
                late = start + SHIFT
                high.append(jnp.concatenate([half[late : late + WINDOW] for half in two], axis=0))
            tokens_ref[at, cols] = jnp.where(side, high[0], low[0]).astype(BF16)
            mine_ref[at, cols] = jnp.where(side, high[1], low[1]).astype(BF16)
            other_ref[at, cols] = jnp.where(side, low[1], high[1]).astype(BF16)


def swiglu_kernel(model, count, parts_ref, packed_ref):
    side = axis_parity("col")
    members = parts_ref.shape[0] // 2

    def summed(parity):
        total = parts_ref[parity].astype(F32)
        for at in range(1, members):
            total = total + parts_ref[2 * at + parity].astype(F32)
        return total

    inner = jnp.zeros((WINDOW, 1), F32)
    inv_rms = None
    for place, parity in enumerate((side, 1 - side)):
        sums = summed(parity)
        gate, up_proj, hidden_grad = sums[:, :SLOT], sums[:, SLOT : 2 * SLOT], sums[:, 2 * SLOT :]
        lane = lax.broadcasted_iota(jnp.int32, gate.shape, 1)
        if place == 0:
            at_squares = (lane >= count) & (lane < count + 2)
            squares = jnp.sum(jnp.where(at_squares, gate, 0.0), axis=1, keepdims=True)
            inv_rms = lax.rsqrt(squares / model + epsilon)
        keep = valid_rows(gate.shape, side) & (lane < count)
        gate = jnp.where(keep, gate * inv_rms, 0.0)
        up_proj = up_proj * inv_rms
        sig = jax.nn.sigmoid(gate)
        hidden = jnp.where(keep, gate * sig * up_proj, 0.0)
        gate_grad = jnp.where(keep, hidden_grad * up_proj * sig * (1.0 + gate * (1.0 - sig)), 0.0)
        up_grad = jnp.where(keep, hidden_grad * gate * sig, 0.0)
        gate_grad, up_grad = gate_grad.astype(BF16), up_grad.astype(BF16)
        inner_term = gate_grad.astype(F32) * gate + up_grad.astype(F32) * up_proj
        inner = inner + jnp.sum(inner_term, axis=1, keepdims=True)
        packed_ref[:, (2 * place) * SLOT : (2 * place + 1) * SLOT] = gate_grad
        packed_ref[:, (2 * place + 1) * SLOT : (2 * place + 2) * SLOT] = up_grad
        packed_ref[:, (4 + place) * SLOT : (5 + place) * SLOT] = hidden.astype(BF16)
    own = packed_ref[:, :SLOT].astype(F32)
    lane = lax.broadcasted_iota(jnp.int32, own.shape, 1)
    for place, value in enumerate((split_wide(inner) + split_wide(inv_rms)) * 2):
        own = jnp.where(lane == count + place, value, own)
    packed_ref[:, :SLOT] = own.astype(BF16)


def input_kernel(
    nt,
    shares,
    feats,
    count,
    packed_ref,
    gate_ref,
    up_ref,
    gate_other_ref,
    up_other_ref,
    tokens_ref,
    out_ref,
):
    base = count % 128
    side = axis_parity("col")
    spot = lax.broadcasted_iota(jnp.int32, (EXTRA, feats), 0) % 4
    tail = packed_ref[:, SLOT - 128 : SLOT].astype(F32)
    lane = lax.broadcasted_iota(jnp.int32, tail.shape, 1)
    at_inv = (lane >= base + 2) & (lane < base + 4)
    inv = jnp.sum(jnp.where(at_inv, tail, 0.0), axis=1, keepdims=True)
    extras = []
    for tok in range(nt):
        piece = tail[tok * WINDOW : (tok + 1) * WINDOW]
        square = jnp.concatenate([piece, jnp.zeros((128 - WINDOW, 128), F32)], axis=0)
        turned = square.T[base : base + EXTRA]
        share = jnp.where(axis_parity("tok") == 1, turned[3:4], turned[2:3]) * (1.0 / shares)
        extras.append(jnp.where(spot == 3, share, turned))
    keep = valid_rows((WINDOW, feats), side)
    step = 2 * feats
    fill = jnp.zeros((SLOT - count, step), BF16)
    for chunk in range(tokens_ref.shape[1] // step):
        at = pl.ds(chunk * step, step)
        term = jnp.zeros((packed_ref.shape[0], step), F32)
        for place, ref in enumerate((gate_ref, up_ref, gate_other_ref, up_other_ref)):
            values = packed_ref[:, place * SLOT : (place + 1) * SLOT]
            weight = jnp.concatenate([ref[:, at], fill], axis=0)
            term = term + jnp.dot(values, weight, preferred_element_type=F32)
        gain_term = jnp.sum(term * (tokens_ref[:, at].astype(F32) * inv), axis=0, keepdims=True)
        for part in range(2):
            cols = slice(part * feats, (part + 1) * feats)
            for tok in range(nt):
                extra = jnp.where(spot == 2, gain_term[:, cols], extras[tok])
                extra = jnp.concatenate([extra] * (WINDOW // EXTRA), axis=0)
                block = jnp.where(keep, term[tok * WINDOW : (tok + 1) * WINDOW, cols], extra)
                out_ref[tok, 2 * chunk + part] = block.astype(BF16)


def down_mine_kernel(hidden_ref, grads_ref, out_ref):
    total = lax.dot_general(hidden_ref[...], grads_ref[...], TN_DIMS, preferred_element_type=F32)
    out_ref[...] = total[: out_ref.shape[0]]


def down_other_kernel(hidden_ref, grads_ref, mine_ref, out_ref):
    total = lax.dot_general(hidden_ref[...], grads_ref[...], TN_DIMS, preferred_element_type=F32)
    out_ref[...] = (total[: out_ref.shape[0]] + mine_ref[...]).astype(BF16)


def copy_kernel(copies, own_ref, out_ref):
    own = own_ref[...].astype(F32)
    gain = jnp.broadcast_to(own[-1:], (EXTRA_SENT, own.shape[1]))
    block = jnp.concatenate([own[:-1], gain], axis=0).astype(BF16)
    for copy in range(copies):
        out_ref[copy] = block


def message_kernel(copies, rows, first_ref, out_ref):
    count = first_ref.shape[0]
    for copy in range(copies):
        for at in range(count):
            out_ref[copy, pl.ds(at * rows, rows), :] = first_ref[at, :rows, :]
        out_ref[copy, count * rows :, :] = first_ref[0, rows:, :]


def final_kernel(model, blocks_ref, tokens_ref, grads_ref, gain_ref, tokens_out_ref, gain_out_ref):
    rows, feats = tokens_ref.shape

    def add(at, sums):
        return (
            sums[0] + blocks_ref[2 * at].astype(F32),
            sums[1] + blocks_ref[2 * at + 1].astype(F32),
        )

    start = (blocks_ref[0].astype(F32), blocks_ref[1].astype(F32))
    low, high = lax.fori_loop(1, blocks_ref.shape[0] // 2, add, start, unroll=True)
    rest = jnp.zeros((feats - EXTRA, feats), F32)
    low_turned = jnp.concatenate([low[SHIFT:], rest], axis=0).T[:WINDOW]
    high_turned = jnp.concatenate([high[:EXTRA], rest], axis=0).T[:WINDOW]
    inner = join_windows(low_turned[:, 4:5] + low_turned[:, 5:6], high_turned[:, 0:1] + high_turned[:, 1:2])
    inner = inner / model
    inv = join_windows(low_turned[:, 7:8], high_turned[:, 3:4])
    gain_out_ref[...] = low[SHIFT + 6 : SHIFT + 7] + high[2:3]
    scaled = tokens_ref[...].astype(F32) * inv
    weighted = join_windows(low, high) * gain_ref[...].astype(F32)
    result = grads_ref[...].astype(F32) + inv * (weighted - scaled * inner)
    tokens_out_ref[...] = result.astype(BF16)


def whole(memory=pltpu.VMEM):
    return pl.BlockSpec(memory_space=memory)


def on_device(tokens, d_out, gain, gate_weight, up_weight, down_weight):
    nt, nr, nc = (lax.axis_size(a) for a in AXES)
    rows, feats = tokens.shape
    count = gate_weight.shape[0]
    width = nc * feats
    model = nr * width

    neighbours = [(at, at ^ 1) for at in range(nc)]
    gain_row = gain.reshape(1, feats)
    tall = 2 * rows + EXTRA_SENT
    copies = pl.pallas_call(
        functools.partial(copy_kernel, nc),
        out_shape=jax.ShapeDtypeStruct((nc, tall, feats), BF16),
        in_specs=[whole()],
        out_specs=whole(),
        compiler_params=SMALL,
        name="own_copies",
    )(jnp.concatenate([tokens, d_out, gain_row], axis=0))
    first = mixed_groups(nt, nr, nc, False)
    stage = lax.all_to_all(copies, AXES, 0, 0, tiled=True, axis_index_groups=first)
    long = nc * 2 * rows + EXTRA_SENT
    copies = pl.pallas_call(
        functools.partial(message_kernel, nt, 2 * rows),
        out_shape=jax.ShapeDtypeStruct((nt, long, feats), BF16),
        in_specs=[whole()],
        out_specs=whole(),
        compiler_params=SMALL,
        name="second_messages",
    )(stage)
    second = mixed_groups(nt, nr, nc, True)
    both = lax.all_to_all(copies, AXES, 0, 0, tiled=True, axis_index_groups=second)

    flops = 2 * nt * rows * width * SLOT
    gate_sent, up_sent, both = lax.optimization_barrier((gate_weight, up_weight, both))
    parts = pl.pallas_call(
        functools.partial(forward_kernel, nt, nc, rows, count),
        out_shape=jax.ShapeDtypeStruct((2 * nt, WINDOW, 3 * SLOT), BF16),
        in_specs=[whole()] * 5,
        out_specs=whole(),
        scratch_shapes=[pltpu.VMEM((nt * rows, width), BF16)] * 2 + [pltpu.VMEM((3, SLOT, width), BF16)],
        compiler_params=LARGE,
        cost_estimate=pl.CostEstimate(flops=3 * flops, bytes_accessed=8 * nt * rows * width, transcendentals=0),
        name="forward_parts",
    )(both, stage, gate_weight, up_weight, down_weight)
    gate_other = lax.ppermute(gate_sent, "col", neighbours)
    up_other = lax.ppermute(up_sent, "col", neighbours)
    pairs = [
        [(tok * nr + row) * nc + 2 * pair + side for row in range(nr) for side in range(2)]
        for tok in range(nt)
        for pair in range(nc // 2)
    ]
    parts = lax.all_to_all(parts, AXES, 0, 0, tiled=True, axis_index_groups=pairs)
    packed = pl.pallas_call(
        functools.partial(swiglu_kernel, model, count),
        out_shape=jax.ShapeDtypeStruct((WINDOW, 6 * SLOT), BF16),
        in_specs=[whole()],
        out_specs=whole(),
        compiler_params=SMALL,
        cost_estimate=pl.CostEstimate(
            flops=40 * WINDOW * SLOT, bytes_accessed=16 * WINDOW * SLOT * nr, transcendentals=2 * WINDOW * SLOT
        ),
        name="swiglu_grads",
    )(parts)
    packed = lax.all_gather(packed, "row", axis=0, tiled=True)

    window_cost = pl.CostEstimate(flops=0, bytes_accessed=8 * nt * rows * width, transcendentals=0)
    tokens_all, grads_mine, grads_other = pl.pallas_call(
        functools.partial(windows_kernel, nt, nc, rows),
        out_shape=(jax.ShapeDtypeStruct((nt * WINDOW, width), BF16),) * 3,
        in_specs=[whole(), whole(pl.ANY)],
        out_specs=(whole(),) * 3,
        compiler_params=SMALL,
        cost_estimate=window_cost,
        name="token_windows",
    )(both, packed)
    blocks = pl.pallas_call(
        functools.partial(input_kernel, nt, nt * nc // 4, feats, count),
        out_shape=jax.ShapeDtypeStruct((nt, nc, WINDOW, feats), BF16),
        in_specs=[whole()] * 6,
        out_specs=whole(),
        compiler_params=LARGE,
        cost_estimate=pl.CostEstimate(flops=2 * flops, bytes_accessed=6 * nt * rows * width, transcendentals=0),
        name="input_grad_blocks",
    )(packed, gate_weight, up_weight, gate_other, up_other, tokens_all)
    blocks_sent = blocks.reshape(nt * nc, WINDOW, feats)
    blocks = lax.all_to_all(blocks_sent, ("tok", "col"), 0, 0, tiled=True)

    hidden_other = lax.ppermute(packed[:, 5 * SLOT :], "col", neighbours)
    half_chunk = width // 2
    down_cost = pl.CostEstimate(flops=flops // 2, bytes_accessed=3 * nt * rows * width, transcendentals=0)
    mine = pl.pallas_call(
        down_mine_kernel,
        out_shape=jax.ShapeDtypeStruct((count, width), F32),
        grid=(2,),
        in_specs=[
            pl.BlockSpec((nt * WINDOW, SLOT), lambda j: (0, 4)),
            pl.BlockSpec((nt * WINDOW, half_chunk), lambda j: (0, j)),
        ],
        out_specs=pl.BlockSpec((count, half_chunk), lambda j: (0, j)),
        compiler_params=LARGE,
        cost_estimate=down_cost,
        name="down_grads_mine",
    )(packed, grads_mine)
    d_down = pl.pallas_call(
        down_other_kernel,
        out_shape=jax.ShapeDtypeStruct((count, width), BF16),
        grid=(2,),
        in_specs=[
            pl.BlockSpec((nt * WINDOW, SLOT), lambda j: (0, 0)),
            pl.BlockSpec((nt * WINDOW, half_chunk), lambda j: (0, j)),
            pl.BlockSpec((count, half_chunk), lambda j: (0, j)),
        ],
        out_specs=pl.BlockSpec((count, half_chunk), lambda j: (0, j)),
        compiler_params=LARGE,
        cost_estimate=down_cost,
        name="down_grads",
    )(hidden_other, grads_other, mine)

    d_tokens, d_gain = pl.pallas_call(
        functools.partial(final_kernel, model),
        out_shape=(
            jax.ShapeDtypeStruct((rows, feats), BF16),
            jax.ShapeDtypeStruct((1, feats), F32),
        ),
        in_specs=[whole()] * 4,
        out_specs=(whole(), whole()),
        compiler_params=SMALL,
        name="token_grads",
    )(blocks, tokens, d_out, gain_row)
    d_gain = d_gain.reshape(feats)
    return (d_tokens, d_gain, d_down)


def solution(mesh):
    placed = (
        P("tok", ("row", "col")),
        P("tok", ("row", "col")),
        P(("row", "col")),
        P(("tok", "col"), "row"),
        P(("tok", "col"), "row"),
        P(("tok", "col"), "row"),
    )
    return jax.shard_map(
        on_device,
        mesh=mesh,
        in_specs=placed,
        out_specs=(P("tok", ("row", "col")), P(("row", "col")), P(("tok", "col"), "row")),
        check_vma=False,
    )
```

```python
import functools

import jax
import jax.numpy as jnp
from jax import lax
from jax.experimental import pallas as pl
from jax.experimental.pallas import tpu as pltpu
from jax.sharding import PartitionSpec as P

epsilon = 1e-05
F32 = jnp.float32
BF16 = jnp.bfloat16
AXES = ("tok", "row", "col")
SLOT = 256
EXTRA = 8
EXTRA_SENT = 16
WINDOW = 40
SHIFT = 32
TN_DIMS = (((0,), (0,)), ((), ()))
NT_DIMS = (((1,), (1,)), ((), ()))
SMALL = pltpu.CompilerParams(vmem_limit_bytes=12 * 1024 * 1024)
WIDE = pltpu.CompilerParams(vmem_limit_bytes=59 * 1024 * 1024)
LARGE = pltpu.CompilerParams(vmem_limit_bytes=24 * 1024 * 1024)


def axis_parity(axis):
    return lax.rem(lax.axis_index(axis), 2)


def split_wide(value):
    high = value.astype(BF16).astype(F32)
    return high, value - high


def mixed_groups(tok_count, row_count, col_count, even_along_tok):
    groups = []
    for row in range(row_count):
        if (row % 2 == 0) == even_along_tok:
            for col in range(col_count):
                groups.append([(tok * row_count + row) * col_count + col for tok in range(tok_count)])
        else:
            for tok in range(tok_count):
                groups.append([(tok * row_count + row) * col_count + col for col in range(col_count)])
    return groups


def padded_weight(ref, scratch):
    count = ref.shape[0]
    scratch[:count, :] = ref[...]
    scratch[count:, :] = jnp.zeros((scratch.shape[0] - count, ref.shape[1]), BF16)
    return scratch[...]


def valid_rows(shape, side):
    row = lax.broadcasted_iota(jnp.int32, shape, 0)
    return (row >= 4 * side) & (row < WINDOW - 4 + 4 * side)


def join_windows(low, high):
    row = lax.broadcasted_iota(jnp.int32, (8,) + low.shape[1:], 0)
    shared = jnp.where(row < 4, low[SHIFT:], high[: WINDOW - SHIFT])
    return jnp.concatenate([low[:SHIFT], shared, high[WINDOW - SHIFT :]], axis=0)


def block_pair(blocks_ref, odd, pair, col, rows):
    two = []
    for tok in (2 * pair, 2 * pair + 1):
        outer, step = jnp.where(odd, col, tok), jnp.where(odd, tok, col)
        start = pl.multiple_of(step * (2 * rows), 16)
        two.append(blocks_ref[outer, pl.ds(start, 2 * rows), :].astype(F32))
    return two


def forward_kernel(
    nt,
    nc,
    rows,
    count,
    blocks_ref,
    first_ref,
    gate_ref,
    up_ref,
    down_ref,
    part_ref,
    grads_ref,
    scaled_ref,
    w_ref,
):
    odd = axis_parity("row") == 1
    feats = blocks_ref.shape[2]
    gains = []
    for col in range(nc):
        late = blocks_ref[col, nt * 2 * rows :, :].astype(F32)
        early = first_ref[col, 2 * rows :, :].astype(F32)
        gains.append(jnp.where(odd, late, early)[0:1])
    totals = []
    for pair in range(nt // 2):
        at = pl.ds(pair * 2 * rows, 2 * rows)
        squares = jnp.zeros((2 * rows, feats), F32)
        for col in range(nc):
            two = block_pair(blocks_ref, odd, pair, col, rows)
            wide = jnp.concatenate([two[0][:rows], two[1][:rows]], axis=0)
            grads = jnp.concatenate([two[0][rows:], two[1][rows:]], axis=0)
            cols = pl.ds(col * feats, feats)
            grads_ref[at, cols] = grads.astype(BF16)
            scaled_ref[at, cols] = (wide * gains[col]).astype(BF16)
            squares = squares + wide * wide
        totals.append(jnp.sum(squares, axis=1, keepdims=True))
    high, low = split_wide(jnp.concatenate(totals, axis=0))
    for place, (source, weight) in enumerate(((scaled_ref, gate_ref), (scaled_ref, up_ref), (grads_ref, down_ref))):
        padded = padded_weight(weight, w_ref.at[place])
        value = lax.dot_general(source[...], padded, NT_DIMS, preferred_element_type=F32)
        if place == 0:
            lane = lax.broadcasted_iota(jnp.int32, value.shape, 1)
            value = jnp.where(lane == count, high, jnp.where(lane == count + 1, low, value))
        cols = pl.ds(place * SLOT, SLOT)
        for tok in range(nt):
            for half in range(2):
                start = tok * rows + half * SHIFT
                part_ref[2 * tok + half, :, cols] = value[start : start + WINDOW].astype(BF16)


def windows_kernel(nt, nc, rows, blocks_ref, after_ref, tokens_ref, mine_ref, other_ref):
    odd = axis_parity("row") == 1
    side = axis_parity("col") == 1
    feats = blocks_ref.shape[2]
    for pair in range(nt // 2):
        at = pl.ds(pair * 2 * WINDOW, 2 * WINDOW)
        for col in range(nc):
            two = block_pair(blocks_ref, odd, pair, col, rows)
            cols = pl.ds(col * feats, feats)
            low, high = [], []
            for start in (0, rows):
                low.append(jnp.concatenate([half[start : start + WINDOW] for half in two], axis=0))
                late = start + SHIFT
                high.append(jnp.concatenate([half[late : late + WINDOW] for half in two], axis=0))
            tokens_ref[at, cols] = jnp.where(side, high[0], low[0]).astype(BF16)
            mine_ref[at, cols] = jnp.where(side, high[1], low[1]).astype(BF16)
            other_ref[at, cols] = jnp.where(side, low[1], high[1]).astype(BF16)


def swiglu_kernel(model, count, parts_ref, packed_ref):
    side = axis_parity("col")
    members = parts_ref.shape[0] // 2

    def summed(parity):
        total = parts_ref[parity].astype(F32)
        for at in range(1, members):
            total = total + parts_ref[2 * at + parity].astype(F32)
        return total

    inner = jnp.zeros((WINDOW, 1), F32)
    inv_rms = None
    for place, parity in enumerate((side, 1 - side)):
        sums = summed(parity)
        gate, up_proj, hidden_grad = sums[:, :SLOT], sums[:, SLOT : 2 * SLOT], sums[:, 2 * SLOT :]
        lane = lax.broadcasted_iota(jnp.int32, gate.shape, 1)
        if place == 0:
            at_squares = (lane >= count) & (lane < count + 2)
            squares = jnp.sum(jnp.where(at_squares, gate, 0.0), axis=1, keepdims=True)
            inv_rms = lax.rsqrt(squares / model + epsilon)
        keep = valid_rows(gate.shape, side) & (lane < count)
        gate = jnp.where(keep, gate * inv_rms, 0.0)
        up_proj = up_proj * inv_rms
        sig = jax.nn.sigmoid(gate)
        hidden = jnp.where(keep, gate * sig * up_proj, 0.0)
        gate_grad = jnp.where(keep, hidden_grad * up_proj * sig * (1.0 + gate * (1.0 - sig)), 0.0)
        up_grad = jnp.where(keep, hidden_grad * gate * sig, 0.0)
        gate_grad, up_grad = gate_grad.astype(BF16), up_grad.astype(BF16)
        inner_term = gate_grad.astype(F32) * gate + up_grad.astype(F32) * up_proj
        inner = inner + jnp.sum(inner_term, axis=1, keepdims=True)
        packed_ref[:, (2 * place) * SLOT : (2 * place + 1) * SLOT] = gate_grad
        packed_ref[:, (2 * place + 1) * SLOT : (2 * place + 2) * SLOT] = up_grad
        packed_ref[:, (4 + place) * SLOT : (5 + place) * SLOT] = hidden.astype(BF16)
    own = packed_ref[:, :SLOT].astype(F32)
    lane = lax.broadcasted_iota(jnp.int32, own.shape, 1)
    for place, value in enumerate((split_wide(inner) + split_wide(inv_rms)) * 2):
        own = jnp.where(lane == count + place, value, own)
    packed_ref[:, :SLOT] = own.astype(BF16)


def weight_columns(ref, at):
    fill = jnp.zeros((SLOT - ref.shape[0], at.size), BF16)
    return jnp.concatenate([ref[:, at], fill], axis=0)


def three_terms_kernel(step, packed_ref, gate_ref, up_ref, gate_other_ref, out_ref):
    for chunk in range(out_ref.shape[1] // step):
        at = pl.ds(chunk * step, step)
        term = jnp.zeros((out_ref.shape[0], step), F32)
        for place, ref in enumerate((gate_ref, up_ref, gate_other_ref)):
            values = packed_ref[:, place * SLOT : (place + 1) * SLOT]
            term = term + jnp.dot(values, weight_columns(ref, at), preferred_element_type=F32)
        out_ref[:, at] = term


def input_kernel(
    nt,
    shares,
    feats,
    count,
    packed_ref,
    three_ref,
    up_other_ref,
    tokens_ref,
    out_ref,
    w_ref,
    block_ref,
    in_sem,
    out_sems,
):
    load = pltpu.make_async_copy(up_other_ref, w_ref.at[pl.ds(0, count)], in_sem)
    load.start()
    w_ref[count:, :] = jnp.zeros((SLOT - count, w_ref.shape[1]), BF16)
    base = count % 128
    side = axis_parity("col")
    spot = lax.broadcasted_iota(jnp.int32, (EXTRA, feats), 0) % 4
    tail = packed_ref[:, SLOT - 128 : SLOT].astype(F32)
    lane = lax.broadcasted_iota(jnp.int32, tail.shape, 1)
    at_inv = (lane >= base + 2) & (lane < base + 4)
    inv = jnp.sum(jnp.where(at_inv, tail, 0.0), axis=1, keepdims=True)
    extras = []
    for tok in range(nt):
        piece = tail[tok * WINDOW : (tok + 1) * WINDOW]
        square = jnp.concatenate([piece, jnp.zeros((128 - WINDOW, 128), F32)], axis=0)
        turned = square.T[base : base + EXTRA]
        share = jnp.where(axis_parity("tok") == 1, turned[3:4], turned[2:3]) * (1.0 / shares)
        extras.append(jnp.where(spot == 3, share, turned))
    keep = valid_rows((WINDOW, feats), side)
    step = 2 * feats
    stores = []
    load.wait()
    for chunk in range(tokens_ref.shape[1] // step):
        at = pl.ds(chunk * step, step)
        values = packed_ref[:, 3 * SLOT : 4 * SLOT]
        term = jnp.dot(values, w_ref[:, at], preferred_element_type=F32) + three_ref[:, at]
        gain_term = jnp.sum(term * (tokens_ref[:, at].astype(F32) * inv), axis=0, keepdims=True)
        for part in range(2):
            cols = slice(part * feats, (part + 1) * feats)
            for tok in range(nt):
                extra = jnp.where(spot == 2, gain_term[:, cols], extras[tok])
                extra = jnp.concatenate([extra] * (WINDOW // EXTRA), axis=0)
                block = jnp.where(keep, term[tok * WINDOW : (tok + 1) * WINDOW, cols], extra)
                block_ref[tok, 2 * chunk + part] = block.astype(BF16)
        two = pl.ds(2 * chunk, 2)
        stores.append(pltpu.make_async_copy(block_ref.at[:, two], out_ref.at[:, two], out_sems.at[chunk]))
        stores[-1].start()
    for store in stores:
        store.wait()


def down_mine_kernel(hidden_ref, grads_ref, out_ref):
    total = lax.dot_general(hidden_ref[...], grads_ref[...], TN_DIMS, preferred_element_type=F32)
    out_ref[...] = total[: out_ref.shape[0]]


def down_other_kernel(hidden_ref, grads_ref, mine_ref, out_ref):
    total = lax.dot_general(hidden_ref[...], grads_ref[...], TN_DIMS, preferred_element_type=F32)
    out_ref[...] = (total[: out_ref.shape[0]] + mine_ref[...]).astype(BF16)


def copy_kernel(copies, own_ref, out_ref):
    own = own_ref[...].astype(F32)
    gain = jnp.broadcast_to(own[-1:], (EXTRA_SENT, own.shape[1]))
    block = jnp.concatenate([own[:-1], gain], axis=0).astype(BF16)
    for copy in range(copies):
        out_ref[copy] = block


def message_kernel(copies, rows, first_ref, out_ref):
    count = first_ref.shape[0]
    for copy in range(copies):
        for at in range(count):
            out_ref[copy, pl.ds(at * rows, rows), :] = first_ref[at, :rows, :]
        out_ref[copy, count * rows :, :] = first_ref[0, rows:, :]


def final_kernel(model, blocks_ref, tokens_ref, grads_ref, gain_ref, tokens_out_ref, gain_out_ref):
    rows, feats = tokens_ref.shape

    def add(at, sums):
        return (
            sums[0] + blocks_ref[2 * at].astype(F32),
            sums[1] + blocks_ref[2 * at + 1].astype(F32),
        )

    start = (blocks_ref[0].astype(F32), blocks_ref[1].astype(F32))
    low, high = lax.fori_loop(1, blocks_ref.shape[0] // 2, add, start, unroll=True)
    rest = jnp.zeros((feats - EXTRA, feats), F32)
    low_turned = jnp.concatenate([low[SHIFT:], rest], axis=0).T[:WINDOW]
    high_turned = jnp.concatenate([high[:EXTRA], rest], axis=0).T[:WINDOW]
    inner = join_windows(low_turned[:, 4:5] + low_turned[:, 5:6], high_turned[:, 0:1] + high_turned[:, 1:2])
    inner = inner / model
    inv = join_windows(low_turned[:, 7:8], high_turned[:, 3:4])
    gain_out_ref[...] = low[SHIFT + 6 : SHIFT + 7] + high[2:3]
    scaled = tokens_ref[...].astype(F32) * inv
    weighted = join_windows(low, high) * gain_ref[...].astype(F32)
    result = grads_ref[...].astype(F32) + inv * (weighted - scaled * inner)
    tokens_out_ref[...] = result.astype(BF16)


def whole(memory=pltpu.VMEM):
    return pl.BlockSpec(memory_space=memory)


def on_device(tokens, d_out, gain, gate_weight, up_weight, down_weight):
    nt, nr, nc = (lax.axis_size(a) for a in AXES)
    rows, feats = tokens.shape
    count = gate_weight.shape[0]
    width = nc * feats
    model = nr * width

    neighbours = [(at, at ^ 1) for at in range(nc)]
    gain_row = gain.reshape(1, feats)
    tall = 2 * rows + EXTRA_SENT
    copies = pl.pallas_call(
        functools.partial(copy_kernel, nc),
        out_shape=jax.ShapeDtypeStruct((nc, tall, feats), BF16),
        in_specs=[whole()],
        out_specs=whole(),
        compiler_params=SMALL,
        name="own_copies",
    )(jnp.concatenate([tokens, d_out, gain_row], axis=0))
    first = mixed_groups(nt, nr, nc, False)
    stage = lax.all_to_all(copies, AXES, 0, 0, tiled=True, axis_index_groups=first)
    long = nc * 2 * rows + EXTRA_SENT
    copies = pl.pallas_call(
        functools.partial(message_kernel, nt, 2 * rows),
        out_shape=jax.ShapeDtypeStruct((nt, long, feats), BF16),
        in_specs=[whole()],
        out_specs=whole(),
        compiler_params=SMALL,
        name="second_messages",
    )(stage)
    second = mixed_groups(nt, nr, nc, True)
    both = lax.all_to_all(copies, AXES, 0, 0, tiled=True, axis_index_groups=second)

    flops = 2 * nt * rows * width * SLOT
    gate_sent, up_sent, both = lax.optimization_barrier((gate_weight, up_weight, both))
    parts = pl.pallas_call(
        functools.partial(forward_kernel, nt, nc, rows, count),
        out_shape=jax.ShapeDtypeStruct((2 * nt, WINDOW, 3 * SLOT), BF16),
        in_specs=[whole()] * 5,
        out_specs=whole(),
        scratch_shapes=[pltpu.VMEM((nt * rows, width), BF16)] * 2 + [pltpu.VMEM((3, SLOT, width), BF16)],
        compiler_params=LARGE,
        cost_estimate=pl.CostEstimate(flops=3 * flops, bytes_accessed=8 * nt * rows * width, transcendentals=0),
        name="forward_parts",
    )(both, stage, gate_weight, up_weight, down_weight)
    gate_other = lax.ppermute(gate_sent, "col", neighbours)
    up_other = lax.ppermute(up_sent, "col", neighbours)
    pairs = [
        [(tok * nr + row) * nc + 2 * pair + side for row in range(nr) for side in range(2)]
        for tok in range(nt)
        for pair in range(nc // 2)
    ]
    parts = lax.all_to_all(parts, AXES, 0, 0, tiled=True, axis_index_groups=pairs)
    packed = pl.pallas_call(
        functools.partial(swiglu_kernel, model, count),
        out_shape=jax.ShapeDtypeStruct((WINDOW, 6 * SLOT), BF16),
        in_specs=[whole()],
        out_specs=whole(),
        compiler_params=SMALL,
        cost_estimate=pl.CostEstimate(
            flops=40 * WINDOW * SLOT, bytes_accessed=16 * WINDOW * SLOT * nr, transcendentals=2 * WINDOW * SLOT
        ),
        name="swiglu_grads",
    )(parts)
    packed = lax.all_gather(packed, "row", axis=0, tiled=True)

    window_cost = pl.CostEstimate(flops=0, bytes_accessed=8 * nt * rows * width, transcendentals=0)
    tokens_all, grads_mine, grads_other = pl.pallas_call(
        functools.partial(windows_kernel, nt, nc, rows),
        out_shape=(jax.ShapeDtypeStruct((nt * WINDOW, width), BF16),) * 3,
        in_specs=[whole(), whole(pl.ANY)],
        out_specs=(whole(),) * 3,
        compiler_params=SMALL,
        cost_estimate=window_cost,
        name="token_windows",
    )(both, packed)
    three = pl.pallas_call(
        functools.partial(three_terms_kernel, 2 * feats),
        out_shape=jax.ShapeDtypeStruct((nt * WINDOW, width), F32),
        in_specs=[whole()] * 4,
        out_specs=whole(),
        compiler_params=LARGE,
        cost_estimate=pl.CostEstimate(flops=flops, bytes_accessed=4 * nt * rows * width, transcendentals=0),
        name="three_terms",
    )(packed, gate_weight, up_weight, gate_other)
    blocks = pl.pallas_call(
        functools.partial(input_kernel, nt, nt * nc // 4, feats, count),
        out_shape=jax.ShapeDtypeStruct((nt, nc, WINDOW, feats), BF16),
        in_specs=[whole(), whole(), whole(pl.ANY), whole()],
        out_specs=whole(pl.ANY),
        scratch_shapes=[
            pltpu.VMEM((SLOT, width), BF16),
            pltpu.VMEM((nt, nc, WINDOW, feats), BF16),
            pltpu.SemaphoreType.DMA(()),
            pltpu.SemaphoreType.DMA((nc // 2,)),
        ],
        compiler_params=LARGE,
        cost_estimate=pl.CostEstimate(flops=flops, bytes_accessed=6 * nt * rows * width, transcendentals=0),
        name="input_grad_blocks",
    )(packed, three, up_other, tokens_all)
    blocks_sent = blocks.reshape(nt * nc, WINDOW, feats)
    blocks = lax.all_to_all(blocks_sent, ("tok", "col"), 0, 0, tiled=True)

    hidden_other = lax.ppermute(packed[:, 5 * SLOT :], "col", neighbours)
    half_chunk = width // 2
    down_cost = pl.CostEstimate(flops=flops // 2, bytes_accessed=3 * nt * rows * width, transcendentals=0)
    mine = pl.pallas_call(
        down_mine_kernel,
        out_shape=jax.ShapeDtypeStruct((count, width), F32),
        grid=(2,),
        in_specs=[
            pl.BlockSpec((nt * WINDOW, SLOT), lambda j: (0, 4)),
            pl.BlockSpec((nt * WINDOW, half_chunk), lambda j: (0, j)),
        ],
        out_specs=pl.BlockSpec((count, half_chunk), lambda j: (0, j)),
        compiler_params=LARGE,
        cost_estimate=down_cost,
        name="down_grads_mine",
    )(packed, grads_mine)
    d_down = pl.pallas_call(
        down_other_kernel,
        out_shape=jax.ShapeDtypeStruct((count, width), BF16),
        grid=(2,),
        in_specs=[
            pl.BlockSpec((nt * WINDOW, SLOT), lambda j: (0, 0)),
            pl.BlockSpec((nt * WINDOW, half_chunk), lambda j: (0, j)),
            pl.BlockSpec((count, half_chunk), lambda j: (0, j)),
        ],
        out_specs=pl.BlockSpec((count, half_chunk), lambda j: (0, j)),
        compiler_params=LARGE,
        cost_estimate=down_cost,
        name="down_grads",
    )(hidden_other, grads_other, mine)

    d_tokens, d_gain = pl.pallas_call(
        functools.partial(final_kernel, model),
        out_shape=(
            jax.ShapeDtypeStruct((rows, feats), BF16),
            jax.ShapeDtypeStruct((1, feats), F32),
        ),
        in_specs=[whole()] * 4,
        out_specs=(whole(), whole()),
        compiler_params=SMALL,
        name="token_grads",
    )(blocks, tokens, d_out, gain_row)
    d_gain = d_gain.reshape(feats)
    return (d_tokens, d_gain, d_down)


def solution(mesh):
    placed = (
        P("tok", ("row", "col")),
        P("tok", ("row", "col")),
        P(("row", "col")),
        P(("tok", "col"), "row"),
        P(("tok", "col"), "row"),
        P(("tok", "col"), "row"),
    )
    return jax.shard_map(
        on_device,
        mesh=mesh,
        in_specs=placed,
        out_specs=(P("tok", ("row", "col")), P(("row", "col")), P(("tok", "col"), "row")),
        check_vma=False,
    )
```

```python
import functools

import jax
import jax.numpy as jnp
from jax import lax
from jax.experimental import pallas as pl
from jax.experimental.pallas import tpu as pltpu
from jax.sharding import PartitionSpec as P

epsilon = 1e-05
F32 = jnp.float32
BF16 = jnp.bfloat16
AXES = ("tok", "row", "col")
SLOT = 256
EXTRA = 8
EXTRA_SENT = 16
WINDOW = 40
SHIFT = 32
TN_DIMS = (((0,), (0,)), ((), ()))
NT_DIMS = (((1,), (1,)), ((), ()))
SMALL = pltpu.CompilerParams(vmem_limit_bytes=12 * 1024 * 1024)
WIDE = pltpu.CompilerParams(vmem_limit_bytes=59 * 1024 * 1024)
LARGE = pltpu.CompilerParams(vmem_limit_bytes=24 * 1024 * 1024)


def axis_parity(axis):
    return lax.rem(lax.axis_index(axis), 2)


def split_wide(value):
    high = value.astype(BF16).astype(F32)
    return high, value - high


def mixed_groups(tok_count, row_count, col_count, even_along_tok):
    groups = []
    for row in range(row_count):
        if (row % 2 == 0) == even_along_tok:
            for col in range(col_count):
                groups.append([(tok * row_count + row) * col_count + col for tok in range(tok_count)])
        else:
            for tok in range(tok_count):
                groups.append([(tok * row_count + row) * col_count + col for col in range(col_count)])
    return groups


def padded_weight(ref, scratch):
    count = ref.shape[0]
    scratch[:count, :] = ref[...]
    scratch[count:, :] = jnp.zeros((scratch.shape[0] - count, ref.shape[1]), BF16)
    return scratch[...]


def valid_rows(shape, side):
    row = lax.broadcasted_iota(jnp.int32, shape, 0)
    return (row >= 4 * side) & (row < WINDOW - 4 + 4 * side)


def join_windows(low, high):
    row = lax.broadcasted_iota(jnp.int32, (8,) + low.shape[1:], 0)
    shared = jnp.where(row < 4, low[SHIFT:], high[: WINDOW - SHIFT])
    return jnp.concatenate([low[:SHIFT], shared, high[WINDOW - SHIFT :]], axis=0)


def block_pair(blocks_ref, odd, pair, col, rows):
    two = []
    for tok in (2 * pair, 2 * pair + 1):
        outer, step = jnp.where(odd, col, tok), jnp.where(odd, tok, col)
        start = pl.multiple_of(step * (2 * rows), 16)
        two.append(blocks_ref[outer, pl.ds(start, 2 * rows), :].astype(F32))
    return two


def forward_kernel(
    nt,
    nc,
    rows,
    count,
    blocks_ref,
    first_ref,
    gate_ref,
    up_ref,
    down_ref,
    part_ref,
    grads_ref,
    scaled_ref,
    w_ref,
):
    odd = axis_parity("row") == 1
    feats = blocks_ref.shape[2]
    gains = []
    for col in range(nc):
        late = blocks_ref[col, nt * 2 * rows :, :].astype(F32)
        early = first_ref[col, 2 * rows :, :].astype(F32)
        gains.append(jnp.where(odd, late, early)[0:1])
    totals = []
    for pair in range(nt // 2):
        at = pl.ds(pair * 2 * rows, 2 * rows)
        squares = jnp.zeros((2 * rows, feats), F32)
        for col in range(nc):
            two = block_pair(blocks_ref, odd, pair, col, rows)
            wide = jnp.concatenate([two[0][:rows], two[1][:rows]], axis=0)
            grads = jnp.concatenate([two[0][rows:], two[1][rows:]], axis=0)
            cols = pl.ds(col * feats, feats)
            grads_ref[at, cols] = grads.astype(BF16)
            scaled_ref[at, cols] = (wide * gains[col]).astype(BF16)
            squares = squares + wide * wide
        totals.append(jnp.sum(squares, axis=1, keepdims=True))
    high, low = split_wide(jnp.concatenate(totals, axis=0))
    for place, (source, weight) in enumerate(((scaled_ref, gate_ref), (scaled_ref, up_ref), (grads_ref, down_ref))):
        padded = padded_weight(weight, w_ref.at[place])
        value = lax.dot_general(source[...], padded, NT_DIMS, preferred_element_type=F32)
        if place == 0:
            lane = lax.broadcasted_iota(jnp.int32, value.shape, 1)
            value = jnp.where(lane == count, high, jnp.where(lane == count + 1, low, value))
        cols = pl.ds(place * SLOT, SLOT)
        for tok in range(nt):
            for half in range(2):
                start = tok * rows + half * SHIFT
                part_ref[2 * tok + half, :, cols] = value[start : start + WINDOW].astype(BF16)


def windows_kernel(nt, nc, rows, blocks_ref, after_ref, tokens_ref, mine_ref, other_ref):
    odd = axis_parity("row") == 1
    side = axis_parity("col") == 1
    feats = blocks_ref.shape[2]
    for pair in range(nt // 2):
        at = pl.ds(pair * 2 * WINDOW, 2 * WINDOW)
        for col in range(nc):
            two = block_pair(blocks_ref, odd, pair, col, rows)
            cols = pl.ds(col * feats, feats)
            low, high = [], []
            for start in (0, rows):
                low.append(jnp.concatenate([half[start : start + WINDOW] for half in two], axis=0))
                late = start + SHIFT
                high.append(jnp.concatenate([half[late : late + WINDOW] for half in two], axis=0))
            tokens_ref[at, cols] = jnp.where(side, high[0], low[0]).astype(BF16)
            mine_ref[at, cols] = jnp.where(side, high[1], low[1]).astype(BF16)
            other_ref[at, cols] = jnp.where(side, low[1], high[1]).astype(BF16)


def swiglu_kernel(model, count, parts_ref, packed_ref):
    side = axis_parity("col")
    members = parts_ref.shape[0] // 2

    def summed(parity):
        total = parts_ref[parity].astype(F32)
        for at in range(1, members):
            total = total + parts_ref[2 * at + parity].astype(F32)
        return total

    inner = jnp.zeros((WINDOW, 1), F32)
    inv_rms = None
    for place, parity in enumerate((side, 1 - side)):
        sums = summed(parity)
        gate, up_proj, hidden_grad = sums[:, :SLOT], sums[:, SLOT : 2 * SLOT], sums[:, 2 * SLOT :]
        lane = lax.broadcasted_iota(jnp.int32, gate.shape, 1)
        if place == 0:
            at_squares = (lane >= count) & (lane < count + 2)
            squares = jnp.sum(jnp.where(at_squares, gate, 0.0), axis=1, keepdims=True)
            inv_rms = lax.rsqrt(squares / model + epsilon)
        keep = valid_rows(gate.shape, side) & (lane < count)
        gate = jnp.where(keep, gate * inv_rms, 0.0)
        up_proj = up_proj * inv_rms
        sig = jax.nn.sigmoid(gate)
        hidden = jnp.where(keep, gate * sig * up_proj, 0.0)
        gate_grad = jnp.where(keep, hidden_grad * up_proj * sig * (1.0 + gate * (1.0 - sig)), 0.0)
        up_grad = jnp.where(keep, hidden_grad * gate * sig, 0.0)
        gate_grad, up_grad = gate_grad.astype(BF16), up_grad.astype(BF16)
        inner_term = gate_grad.astype(F32) * gate + up_grad.astype(F32) * up_proj
        inner = inner + jnp.sum(inner_term, axis=1, keepdims=True)
        packed_ref[:, (2 * place) * SLOT : (2 * place + 1) * SLOT] = gate_grad
        packed_ref[:, (2 * place + 1) * SLOT : (2 * place + 2) * SLOT] = up_grad
        packed_ref[:, (4 + place) * SLOT : (5 + place) * SLOT] = hidden.astype(BF16)
    own = packed_ref[:, :SLOT].astype(F32)
    lane = lax.broadcasted_iota(jnp.int32, own.shape, 1)
    for place, value in enumerate((split_wide(inner) + split_wide(inv_rms)) * 2):
        own = jnp.where(lane == count + place, value, own)
    packed_ref[:, :SLOT] = own.astype(BF16)


def weight_columns(ref, at):
    fill = jnp.zeros((SLOT - ref.shape[0], at.size), BF16)
    return jnp.concatenate([ref[:, at], fill], axis=0)


def three_terms_kernel(step, packed_ref, gate_ref, up_ref, gate_other_ref, out_ref):
    for chunk in range(out_ref.shape[1] // step):
        at = pl.ds(chunk * step, step)
        term = jnp.zeros((out_ref.shape[0], step), F32)
        for place, ref in enumerate((gate_ref, up_ref, gate_other_ref)):
            values = packed_ref[:, place * SLOT : (place + 1) * SLOT]
            term = term + jnp.dot(values, weight_columns(ref, at), preferred_element_type=F32)
        out_ref[:, at] = term


def input_kernel(
    nt,
    shares,
    feats,
    count,
    packed_ref,
    three_ref,
    up_other_ref,
    tokens_ref,
    out_ref,
    w_ref,
    block_ref,
    in_sem,
    out_sems,
):
    load = pltpu.make_async_copy(up_other_ref, w_ref.at[pl.ds(0, count)], in_sem)
    load.start()
    w_ref[count:, :] = jnp.zeros((SLOT - count, w_ref.shape[1]), BF16)
    base = count % 128
    side = axis_parity("col")
    spot = lax.broadcasted_iota(jnp.int32, (EXTRA, feats), 0) % 4
    tail = packed_ref[:, SLOT - 128 : SLOT].astype(F32)
    lane = lax.broadcasted_iota(jnp.int32, tail.shape, 1)
    at_inv = (lane >= base + 2) & (lane < base + 4)
    inv = jnp.sum(jnp.where(at_inv, tail, 0.0), axis=1, keepdims=True)
    extras = []
    for tok in range(nt):
        piece = tail[tok * WINDOW : (tok + 1) * WINDOW]
        square = jnp.concatenate([piece, jnp.zeros((128 - WINDOW, 128), F32)], axis=0)
        turned = square.T[base : base + EXTRA]
        share = jnp.where(axis_parity("tok") == 1, turned[3:4], turned[2:3]) * (1.0 / shares)
        extras.append(jnp.where(spot == 3, share, turned))
    keep = valid_rows((WINDOW, feats), side)
    step = 2 * feats
    stores = []
    load.wait()
    for chunk in range(tokens_ref.shape[1] // step):
        at = pl.ds(chunk * step, step)
        values = packed_ref[:, 3 * SLOT : 4 * SLOT]
        term = jnp.dot(values, w_ref[:, at], preferred_element_type=F32) + three_ref[:, at]
        gain_term = jnp.sum(term * (tokens_ref[:, at].astype(F32) * inv), axis=0, keepdims=True)
        for part in range(2):
            cols = slice(part * feats, (part + 1) * feats)
            for tok in range(nt):
                extra = jnp.where(spot == 2, gain_term[:, cols], extras[tok])
                extra = jnp.concatenate([extra] * (WINDOW // EXTRA), axis=0)
                block = jnp.where(keep, term[tok * WINDOW : (tok + 1) * WINDOW, cols], extra)
                block_ref[tok, 2 * chunk + part] = block.astype(BF16)
        two = pl.ds(2 * chunk, 2)
        stores.append(pltpu.make_async_copy(block_ref.at[:, two], out_ref.at[:, two], out_sems.at[chunk]))
        stores[-1].start()
    for store in stores:
        store.wait()


def down_mine_kernel(packed_ref, grads_ref, out_ref):
    hidden = packed_ref[:, 4 * SLOT : 5 * SLOT]
    total = lax.dot_general(hidden, grads_ref[...], TN_DIMS, preferred_element_type=F32)
    out_ref[...] = total[: out_ref.shape[0]]


def down_other_kernel(hidden_ref, grads_ref, mine_ref, out_ref):
    total = lax.dot_general(hidden_ref[...], grads_ref[...], TN_DIMS, preferred_element_type=F32)
    out_ref[...] = (total[: out_ref.shape[0]] + mine_ref[...]).astype(BF16)


def copy_kernel(copies, own_ref, out_ref):
    own = own_ref[...].astype(F32)
    gain = jnp.broadcast_to(own[-1:], (EXTRA_SENT, own.shape[1]))
    block = jnp.concatenate([own[:-1], gain], axis=0).astype(BF16)
    for copy in range(copies):
        out_ref[copy] = block


def message_kernel(copies, rows, first_ref, out_ref):
    count = first_ref.shape[0]
    for copy in range(copies):
        for at in range(count):
            out_ref[copy, pl.ds(at * rows, rows), :] = first_ref[at, :rows, :]
        out_ref[copy, count * rows :, :] = first_ref[0, rows:, :]


def final_kernel(model, blocks_ref, tokens_ref, grads_ref, gain_ref, tokens_out_ref, gain_out_ref):
    rows, feats = tokens_ref.shape

    def add(at, sums):
        return (
            sums[0] + blocks_ref[2 * at].astype(F32),
            sums[1] + blocks_ref[2 * at + 1].astype(F32),
        )

    start = (blocks_ref[0].astype(F32), blocks_ref[1].astype(F32))
    low, high = lax.fori_loop(1, blocks_ref.shape[0] // 2, add, start, unroll=True)
    rest = jnp.zeros((feats - EXTRA, feats), F32)
    low_turned = jnp.concatenate([low[SHIFT:], rest], axis=0).T[:WINDOW]
    high_turned = jnp.concatenate([high[:EXTRA], rest], axis=0).T[:WINDOW]
    inner = join_windows(low_turned[:, 4:5] + low_turned[:, 5:6], high_turned[:, 0:1] + high_turned[:, 1:2])
    inner = inner / model
    inv = join_windows(low_turned[:, 7:8], high_turned[:, 3:4])
    gain_out_ref[...] = low[SHIFT + 6 : SHIFT + 7] + high[2:3]
    scaled = tokens_ref[...].astype(F32) * inv
    weighted = join_windows(low, high) * gain_ref[...].astype(F32)
    result = grads_ref[...].astype(F32) + inv * (weighted - scaled * inner)
    tokens_out_ref[...] = result.astype(BF16)


def whole(memory=pltpu.VMEM):
    return pl.BlockSpec(memory_space=memory)


def on_device(tokens, d_out, gain, gate_weight, up_weight, down_weight):
    nt, nr, nc = (lax.axis_size(a) for a in AXES)
    rows, feats = tokens.shape
    count = gate_weight.shape[0]
    width = nc * feats
    model = nr * width

    neighbours = [(at, at ^ 1) for at in range(nc)]
    gain_row = gain.reshape(1, feats)
    tall = 2 * rows + EXTRA_SENT
    copies = pl.pallas_call(
        functools.partial(copy_kernel, nc),
        out_shape=jax.ShapeDtypeStruct((nc, tall, feats), BF16),
        in_specs=[whole()],
        out_specs=whole(),
        compiler_params=SMALL,
        name="own_copies",
    )(jnp.concatenate([tokens, d_out, gain_row], axis=0))
    first = mixed_groups(nt, nr, nc, False)
    stage = lax.all_to_all(copies, AXES, 0, 0, tiled=True, axis_index_groups=first)
    long = nc * 2 * rows + EXTRA_SENT
    copies = pl.pallas_call(
        functools.partial(message_kernel, nt, 2 * rows),
        out_shape=jax.ShapeDtypeStruct((nt, long, feats), BF16),
        in_specs=[whole()],
        out_specs=whole(),
        compiler_params=SMALL,
        name="second_messages",
    )(stage)
    second = mixed_groups(nt, nr, nc, True)
    both = lax.all_to_all(copies, AXES, 0, 0, tiled=True, axis_index_groups=second)

    flops = 2 * nt * rows * width * SLOT
    gate_sent, up_sent, both = lax.optimization_barrier((gate_weight, up_weight, both))
    parts = pl.pallas_call(
        functools.partial(forward_kernel, nt, nc, rows, count),
        out_shape=jax.ShapeDtypeStruct((2 * nt, WINDOW, 3 * SLOT), BF16),
        in_specs=[whole()] * 5,
        out_specs=whole(),
        scratch_shapes=[pltpu.VMEM((nt * rows, width), BF16)] * 2 + [pltpu.VMEM((3, SLOT, width), BF16)],
        compiler_params=LARGE,
        cost_estimate=pl.CostEstimate(flops=3 * flops, bytes_accessed=8 * nt * rows * width, transcendentals=0),
        name="forward_parts",
    )(both, stage, gate_weight, up_weight, down_weight)
    gate_other = lax.ppermute(gate_sent, "col", neighbours)
    up_other = lax.ppermute(up_sent, "col", neighbours)
    pairs = [
        [(tok * nr + row) * nc + 2 * pair + side for row in range(nr) for side in range(2)]
        for tok in range(nt)
        for pair in range(nc // 2)
    ]
    parts = lax.all_to_all(parts, AXES, 0, 0, tiled=True, axis_index_groups=pairs)
    packed = pl.pallas_call(
        functools.partial(swiglu_kernel, model, count),
        out_shape=jax.ShapeDtypeStruct((WINDOW, 6 * SLOT), BF16),
        in_specs=[whole()],
        out_specs=whole(),
        compiler_params=SMALL,
        cost_estimate=pl.CostEstimate(
            flops=40 * WINDOW * SLOT, bytes_accessed=16 * WINDOW * SLOT * nr, transcendentals=2 * WINDOW * SLOT
        ),
        name="swiglu_grads",
    )(parts)
    packed = lax.all_gather(packed, "row", axis=0, tiled=True)

    window_cost = pl.CostEstimate(flops=0, bytes_accessed=8 * nt * rows * width, transcendentals=0)
    tokens_all, grads_mine, grads_other = pl.pallas_call(
        functools.partial(windows_kernel, nt, nc, rows),
        out_shape=(jax.ShapeDtypeStruct((nt * WINDOW, width), BF16),) * 3,
        in_specs=[whole(), whole(pl.ANY)],
        out_specs=(whole(),) * 3,
        compiler_params=SMALL,
        cost_estimate=window_cost,
        name="token_windows",
    )(both, packed)
    three = pl.pallas_call(
        functools.partial(three_terms_kernel, 2 * feats),
        out_shape=jax.ShapeDtypeStruct((nt * WINDOW, width), F32),
        in_specs=[whole()] * 4,
        out_specs=whole(),
        compiler_params=LARGE,
        cost_estimate=pl.CostEstimate(flops=flops, bytes_accessed=4 * nt * rows * width, transcendentals=0),
        name="three_terms",
    )(packed, gate_weight, up_weight, gate_other)
    blocks = pl.pallas_call(
        functools.partial(input_kernel, nt, nt * nc // 4, feats, count),
        out_shape=jax.ShapeDtypeStruct((nt, nc, WINDOW, feats), BF16),
        in_specs=[whole(), whole(), whole(pl.ANY), whole()],
        out_specs=whole(pl.ANY),
        scratch_shapes=[
            pltpu.VMEM((SLOT, width), BF16),
            pltpu.VMEM((nt, nc, WINDOW, feats), BF16),
            pltpu.SemaphoreType.DMA(()),
            pltpu.SemaphoreType.DMA((nc // 2,)),
        ],
        compiler_params=LARGE,
        cost_estimate=pl.CostEstimate(flops=flops, bytes_accessed=6 * nt * rows * width, transcendentals=0),
        name="input_grad_blocks",
    )(packed, three, up_other, tokens_all)
    blocks_sent = blocks.reshape(nt * nc, WINDOW, feats)
    blocks = lax.all_to_all(blocks_sent, ("tok", "col"), 0, 0, tiled=True)

    hidden_other = lax.ppermute(packed[:, 5 * SLOT :], "col", neighbours)
    down_cost = pl.CostEstimate(flops=flops // 2, bytes_accessed=3 * nt * rows * width, transcendentals=0)
    mine = pl.pallas_call(
        down_mine_kernel,
        out_shape=jax.ShapeDtypeStruct((count, width), F32),
        in_specs=[whole()] * 2,
        out_specs=whole(),
        compiler_params=LARGE,
        cost_estimate=down_cost,
        name="down_grads_mine",
    )(packed, grads_mine)
    d_down = pl.pallas_call(
        down_other_kernel,
        out_shape=jax.ShapeDtypeStruct((count, width), BF16),
        in_specs=[whole()] * 3,
        out_specs=whole(),
        compiler_params=LARGE,
        cost_estimate=down_cost,
        name="down_grads",
    )(hidden_other, grads_other, mine)

    d_tokens, d_gain = pl.pallas_call(
        functools.partial(final_kernel, model),
        out_shape=(
            jax.ShapeDtypeStruct((rows, feats), BF16),
            jax.ShapeDtypeStruct((1, feats), F32),
        ),
        in_specs=[whole()] * 4,
        out_specs=(whole(), whole()),
        compiler_params=SMALL,
        name="token_grads",
    )(blocks, tokens, d_out, gain_row)
    d_gain = d_gain.reshape(feats)
    return (d_tokens, d_gain, d_down)


def solution(mesh):
    placed = (
        P("tok", ("row", "col")),
        P("tok", ("row", "col")),
        P(("row", "col")),
        P(("tok", "col"), "row"),
        P(("tok", "col"), "row"),
        P(("tok", "col"), "row"),
    )
    return jax.shard_map(
        on_device,
        mesh=mesh,
        in_specs=placed,
        out_specs=(P("tok", ("row", "col")), P(("row", "col")), P(("tok", "col"), "row")),
        check_vma=False,
    )
```

```python
import functools

import jax
import jax.numpy as jnp
from jax import lax
from jax.experimental import pallas as pl
from jax.experimental.pallas import tpu as pltpu
from jax.sharding import PartitionSpec as P

epsilon = 1e-05
F32 = jnp.float32
BF16 = jnp.bfloat16
AXES = ("tok", "row", "col")
SLOT = 256
EXTRA = 8
EXTRA_SENT = 16
WINDOW = 40
SHIFT = 32
TN_DIMS = (((0,), (0,)), ((), ()))
NT_DIMS = (((1,), (1,)), ((), ()))
SMALL = pltpu.CompilerParams(vmem_limit_bytes=12 * 1024 * 1024)
WIDE = pltpu.CompilerParams(vmem_limit_bytes=59 * 1024 * 1024)
LARGE = pltpu.CompilerParams(vmem_limit_bytes=24 * 1024 * 1024)


def axis_parity(axis):
    return lax.rem(lax.axis_index(axis), 2)


def split_wide(value):
    high = value.astype(BF16).astype(F32)
    return high, value - high


def mixed_groups(tok_count, row_count, col_count, even_along_tok):
    groups = []
    for row in range(row_count):
        if (row % 2 == 0) == even_along_tok:
            for col in range(col_count):
                groups.append([(tok * row_count + row) * col_count + col for tok in range(tok_count)])
        else:
            for tok in range(tok_count):
                groups.append([(tok * row_count + row) * col_count + col for col in range(col_count)])
    return groups


def padded_weight(ref, scratch):
    count = ref.shape[0]
    scratch[:count, :] = ref[...]
    scratch[count:, :] = jnp.zeros((scratch.shape[0] - count, ref.shape[1]), BF16)
    return scratch[...]


def valid_rows(shape, side):
    row = lax.broadcasted_iota(jnp.int32, shape, 0)
    return (row >= 4 * side) & (row < WINDOW - 4 + 4 * side)


def join_windows(low, high):
    row = lax.broadcasted_iota(jnp.int32, (8,) + low.shape[1:], 0)
    shared = jnp.where(row < 4, low[SHIFT:], high[: WINDOW - SHIFT])
    return jnp.concatenate([low[:SHIFT], shared, high[WINDOW - SHIFT :]], axis=0)


def block_pair(blocks_ref, odd, pair, col, rows):
    two = []
    for tok in (2 * pair, 2 * pair + 1):
        outer, step = jnp.where(odd, col, tok), jnp.where(odd, tok, col)
        start = pl.multiple_of(step * (2 * rows), 16)
        two.append(blocks_ref[outer, pl.ds(start, 2 * rows), :].astype(F32))
    return two


def forward_kernel(
    nt,
    nc,
    rows,
    count,
    blocks_ref,
    first_ref,
    gate_ref,
    up_ref,
    down_ref,
    part_ref,
    grads_ref,
    scaled_ref,
    w_ref,
):
    odd = axis_parity("row") == 1
    feats = blocks_ref.shape[2]
    gains = []
    for col in range(nc):
        late = blocks_ref[col, nt * 2 * rows :, :].astype(F32)
        early = first_ref[col, 2 * rows :, :].astype(F32)
        gains.append(jnp.where(odd, late, early)[0:1])
    totals = []
    for pair in range(nt // 2):
        at = pl.ds(pair * 2 * rows, 2 * rows)
        squares = jnp.zeros((2 * rows, feats), F32)
        for col in range(nc):
            two = block_pair(blocks_ref, odd, pair, col, rows)
            wide = jnp.concatenate([two[0][:rows], two[1][:rows]], axis=0)
            grads = jnp.concatenate([two[0][rows:], two[1][rows:]], axis=0)
            cols = pl.ds(col * feats, feats)
            grads_ref[at, cols] = grads.astype(BF16)
            scaled_ref[at, cols] = (wide * gains[col]).astype(BF16)
            squares = squares + wide * wide
        totals.append(jnp.sum(squares, axis=1, keepdims=True))
    high, low = split_wide(jnp.concatenate(totals, axis=0))
    for place, (source, weight) in enumerate(((scaled_ref, gate_ref), (scaled_ref, up_ref), (grads_ref, down_ref))):
        padded = padded_weight(weight, w_ref.at[place])
        value = lax.dot_general(source[...], padded, NT_DIMS, preferred_element_type=F32)
        if place == 0:
            lane = lax.broadcasted_iota(jnp.int32, value.shape, 1)
            value = jnp.where(lane == count, high, jnp.where(lane == count + 1, low, value))
        cols = pl.ds(place * SLOT, SLOT)
        for tok in range(nt):
            for half in range(2):
                start = tok * rows + half * SHIFT
                part_ref[2 * tok + half, :, cols] = value[start : start + WINDOW].astype(BF16)


def windows_kernel(nt, nc, rows, blocks_ref, after_ref, tokens_ref, mine_ref, other_ref):
    odd = axis_parity("row") == 1
    side = axis_parity("col") == 1
    feats = blocks_ref.shape[2]
    for pair in range(nt // 2):
        at = pl.ds(pair * 2 * WINDOW, 2 * WINDOW)
        for col in range(nc):
            two = block_pair(blocks_ref, odd, pair, col, rows)
            cols = pl.ds(col * feats, feats)
            low, high = [], []
            for start in (0, rows):
                low.append(jnp.concatenate([half[start : start + WINDOW] for half in two], axis=0))
                late = start + SHIFT
                high.append(jnp.concatenate([half[late : late + WINDOW] for half in two], axis=0))
            tokens_ref[at, cols] = jnp.where(side, high[0], low[0]).astype(BF16)
            mine_ref[at, cols] = jnp.where(side, high[1], low[1]).astype(BF16)
            other_ref[at, cols] = jnp.where(side, low[1], high[1]).astype(BF16)


def swiglu_kernel(model, count, parts_ref, packed_ref):
    side = axis_parity("col")
    members = parts_ref.shape[0] // 2

    def summed(parity):
        total = parts_ref[parity].astype(F32)
        for at in range(1, members):
            total = total + parts_ref[2 * at + parity].astype(F32)
        return total

    inner = jnp.zeros((WINDOW, 1), F32)
    inv_rms = None
    for place, parity in enumerate((side, 1 - side)):
        sums = summed(parity)
        gate, up_proj, hidden_grad = sums[:, :SLOT], sums[:, SLOT : 2 * SLOT], sums[:, 2 * SLOT :]
        lane = lax.broadcasted_iota(jnp.int32, gate.shape, 1)
        if place == 0:
            at_squares = (lane >= count) & (lane < count + 2)
            squares = jnp.sum(jnp.where(at_squares, gate, 0.0), axis=1, keepdims=True)
            inv_rms = lax.rsqrt(squares / model + epsilon)
        keep = valid_rows(gate.shape, side) & (lane < count)
        gate = jnp.where(keep, gate * inv_rms, 0.0)
        up_proj = up_proj * inv_rms
        sig = jax.nn.sigmoid(gate)
        hidden = jnp.where(keep, gate * sig * up_proj, 0.0)
        gate_grad = jnp.where(keep, hidden_grad * up_proj * sig * (1.0 + gate * (1.0 - sig)), 0.0)
        up_grad = jnp.where(keep, hidden_grad * gate * sig, 0.0)
        gate_grad, up_grad = gate_grad.astype(BF16), up_grad.astype(BF16)
        inner_term = gate_grad.astype(F32) * gate + up_grad.astype(F32) * up_proj
        inner = inner + jnp.sum(inner_term, axis=1, keepdims=True)
        packed_ref[:, (2 * place) * SLOT : (2 * place + 1) * SLOT] = gate_grad
        packed_ref[:, (2 * place + 1) * SLOT : (2 * place + 2) * SLOT] = up_grad
        packed_ref[:, (4 + place) * SLOT : (5 + place) * SLOT] = hidden.astype(BF16)
    own = packed_ref[:, :SLOT].astype(F32)
    lane = lax.broadcasted_iota(jnp.int32, own.shape, 1)
    for place, value in enumerate((split_wide(inner) + split_wide(inv_rms)) * 2):
        own = jnp.where(lane == count + place, value, own)
    packed_ref[:, :SLOT] = own.astype(BF16)


def weight_columns(ref, at):
    fill = jnp.zeros((SLOT - ref.shape[0], at.size), BF16)
    return jnp.concatenate([ref[:, at], fill], axis=0)


def three_terms_kernel(nt, shares, count, step, packed_ref, gate_ref, up_ref, gate_other_ref, out_ref, extra_ref):
    base = count % 128
    spot = lax.broadcasted_iota(jnp.int32, (EXTRA, 128), 0) % 4
    tail = packed_ref[:, SLOT - 128 : SLOT].astype(F32)
    for tok in range(nt):
        piece = tail[tok * WINDOW : (tok + 1) * WINDOW]
        square = jnp.concatenate([piece, jnp.zeros((128 - WINDOW, 128), F32)], axis=0)
        turned = square.T[base : base + EXTRA]
        share = jnp.where(axis_parity("tok") == 1, turned[3:4], turned[2:3]) * (1.0 / shares)
        extra_ref[tok] = jnp.where(spot == 3, share, turned)
    for chunk in range(out_ref.shape[1] // step):
        at = pl.ds(chunk * step, step)
        term = jnp.zeros((out_ref.shape[0], step), F32)
        for place, ref in enumerate((gate_ref, up_ref, gate_other_ref)):
            values = packed_ref[:, place * SLOT : (place + 1) * SLOT]
            term = term + jnp.dot(values, weight_columns(ref, at), preferred_element_type=F32)
        out_ref[:, at] = term


def input_kernel(
    nt,
    feats,
    count,
    packed_ref,
    three_ref,
    extra_ref,
    up_other_ref,
    tokens_ref,
    out_ref,
    w_ref,
    block_ref,
    in_sem,
    out_sems,
):
    load = pltpu.make_async_copy(up_other_ref, w_ref.at[pl.ds(0, count)], in_sem)
    load.start()
    w_ref[count:, :] = jnp.zeros((SLOT - count, w_ref.shape[1]), BF16)
    base = count % 128
    side = axis_parity("col")
    spot = lax.broadcasted_iota(jnp.int32, (EXTRA, feats), 0) % 4
    tail = packed_ref[:, SLOT - 128 : SLOT].astype(F32)
    lane = lax.broadcasted_iota(jnp.int32, tail.shape, 1)
    at_inv = (lane >= base + 2) & (lane < base + 4)
    inv = jnp.sum(jnp.where(at_inv, tail, 0.0), axis=1, keepdims=True)
    keep = valid_rows((WINDOW, feats), side)
    step = 2 * feats
    stores = []
    load.wait()
    for chunk in range(tokens_ref.shape[1] // step):
        at = pl.ds(chunk * step, step)
        values = packed_ref[:, 3 * SLOT : 4 * SLOT]
        term = jnp.dot(values, w_ref[:, at], preferred_element_type=F32) + three_ref[:, at]
        gain_term = jnp.sum(term * (tokens_ref[:, at].astype(F32) * inv), axis=0, keepdims=True)
        for part in range(2):
            cols = slice(part * feats, (part + 1) * feats)
            for tok in range(nt):
                extra = jnp.where(spot == 2, gain_term[:, cols], extra_ref[tok])
                extra = jnp.concatenate([extra] * (WINDOW // EXTRA), axis=0)
                block = jnp.where(keep, term[tok * WINDOW : (tok + 1) * WINDOW, cols], extra)
                block_ref[tok, 2 * chunk + part] = block.astype(BF16)
        two = pl.ds(2 * chunk, 2)
        stores.append(pltpu.make_async_copy(block_ref.at[:, two], out_ref.at[:, two], out_sems.at[chunk]))
        stores[-1].start()
    for store in stores:
        store.wait()


def down_mine_kernel(packed_ref, grads_ref, out_ref):
    hidden = packed_ref[:, 4 * SLOT : 5 * SLOT]
    total = lax.dot_general(hidden, grads_ref[...], TN_DIMS, preferred_element_type=F32)
    out_ref[...] = total[: out_ref.shape[0]]


def down_other_kernel(hidden_ref, grads_ref, mine_ref, out_ref):
    total = lax.dot_general(hidden_ref[...], grads_ref[...], TN_DIMS, preferred_element_type=F32)
    out_ref[...] = (total[: out_ref.shape[0]] + mine_ref[...]).astype(BF16)


def copy_kernel(copies, own_ref, out_ref):
    own = own_ref[...].astype(F32)
    gain = jnp.broadcast_to(own[-1:], (EXTRA_SENT, own.shape[1]))
    block = jnp.concatenate([own[:-1], gain], axis=0).astype(BF16)
    for copy in range(copies):
        out_ref[copy] = block


def message_kernel(copies, rows, first_ref, out_ref):
    count = first_ref.shape[0]
    for copy in range(copies):
        for at in range(count):
            out_ref[copy, pl.ds(at * rows, rows), :] = first_ref[at, :rows, :]
        out_ref[copy, count * rows :, :] = first_ref[0, rows:, :]


def final_kernel(model, blocks_ref, tokens_ref, grads_ref, gain_ref, tokens_out_ref, gain_out_ref):
    rows, feats = tokens_ref.shape

    def add(at, sums):
        return (
            sums[0] + blocks_ref[2 * at].astype(F32),
            sums[1] + blocks_ref[2 * at + 1].astype(F32),
        )

    start = (blocks_ref[0].astype(F32), blocks_ref[1].astype(F32))
    low, high = lax.fori_loop(1, blocks_ref.shape[0] // 2, add, start, unroll=True)
    rest = jnp.zeros((feats - EXTRA, feats), F32)
    low_turned = jnp.concatenate([low[SHIFT:], rest], axis=0).T[:WINDOW]
    high_turned = jnp.concatenate([high[:EXTRA], rest], axis=0).T[:WINDOW]
    inner = join_windows(low_turned[:, 4:5] + low_turned[:, 5:6], high_turned[:, 0:1] + high_turned[:, 1:2])
    inner = inner / model
    inv = join_windows(low_turned[:, 7:8], high_turned[:, 3:4])
    gain_out_ref[...] = low[SHIFT + 6 : SHIFT + 7] + high[2:3]
    scaled = tokens_ref[...].astype(F32) * inv
    weighted = join_windows(low, high) * gain_ref[...].astype(F32)
    result = grads_ref[...].astype(F32) + inv * (weighted - scaled * inner)
    tokens_out_ref[...] = result.astype(BF16)


def whole(memory=pltpu.VMEM):
    return pl.BlockSpec(memory_space=memory)


def on_device(tokens, d_out, gain, gate_weight, up_weight, down_weight):
    nt, nr, nc = (lax.axis_size(a) for a in AXES)
    rows, feats = tokens.shape
    count = gate_weight.shape[0]
    width = nc * feats
    model = nr * width

    neighbours = [(at, at ^ 1) for at in range(nc)]
    gain_row = gain.reshape(1, feats)
    tall = 2 * rows + EXTRA_SENT
    copies = pl.pallas_call(
        functools.partial(copy_kernel, nc),
        out_shape=jax.ShapeDtypeStruct((nc, tall, feats), BF16),
        in_specs=[whole()],
        out_specs=whole(),
        compiler_params=SMALL,
        name="own_copies",
    )(jnp.concatenate([tokens, d_out, gain_row], axis=0))
    first = mixed_groups(nt, nr, nc, False)
    stage = lax.all_to_all(copies, AXES, 0, 0, tiled=True, axis_index_groups=first)
    long = nc * 2 * rows + EXTRA_SENT
    copies = pl.pallas_call(
        functools.partial(message_kernel, nt, 2 * rows),
        out_shape=jax.ShapeDtypeStruct((nt, long, feats), BF16),
        in_specs=[whole()],
        out_specs=whole(),
        compiler_params=SMALL,
        name="second_messages",
    )(stage)
    second = mixed_groups(nt, nr, nc, True)
    both = lax.all_to_all(copies, AXES, 0, 0, tiled=True, axis_index_groups=second)

    flops = 2 * nt * rows * width * SLOT
    gate_sent, up_sent, both = lax.optimization_barrier((gate_weight, up_weight, both))
    parts = pl.pallas_call(
        functools.partial(forward_kernel, nt, nc, rows, count),
        out_shape=jax.ShapeDtypeStruct((2 * nt, WINDOW, 3 * SLOT), BF16),
        in_specs=[whole()] * 5,
        out_specs=whole(),
        scratch_shapes=[pltpu.VMEM((nt * rows, width), BF16)] * 2 + [pltpu.VMEM((3, SLOT, width), BF16)],
        compiler_params=LARGE,
        cost_estimate=pl.CostEstimate(flops=3 * flops, bytes_accessed=8 * nt * rows * width, transcendentals=0),
        name="forward_parts",
    )(both, stage, gate_weight, up_weight, down_weight)
    gate_other = lax.ppermute(gate_sent, "col", neighbours)
    up_other = lax.ppermute(up_sent, "col", neighbours)
    pairs = [
        [(tok * nr + row) * nc + 2 * pair + side for row in range(nr) for side in range(2)]
        for tok in range(nt)
        for pair in range(nc // 2)
    ]
    parts = lax.all_to_all(parts, AXES, 0, 0, tiled=True, axis_index_groups=pairs)
    packed = pl.pallas_call(
        functools.partial(swiglu_kernel, model, count),
        out_shape=jax.ShapeDtypeStruct((WINDOW, 6 * SLOT), BF16),
        in_specs=[whole()],
        out_specs=whole(),
        compiler_params=SMALL,
        cost_estimate=pl.CostEstimate(
            flops=40 * WINDOW * SLOT, bytes_accessed=16 * WINDOW * SLOT * nr, transcendentals=2 * WINDOW * SLOT
        ),
        name="swiglu_grads",
    )(parts)
    packed = lax.all_gather(packed, "row", axis=0, tiled=True)

    window_cost = pl.CostEstimate(flops=0, bytes_accessed=8 * nt * rows * width, transcendentals=0)
    tokens_all, grads_mine, grads_other = pl.pallas_call(
        functools.partial(windows_kernel, nt, nc, rows),
        out_shape=(jax.ShapeDtypeStruct((nt * WINDOW, width), BF16),) * 3,
        in_specs=[whole(), whole(pl.ANY)],
        out_specs=(whole(),) * 3,
        compiler_params=SMALL,
        cost_estimate=window_cost,
        name="token_windows",
    )(both, packed)
    three, extras = pl.pallas_call(
        functools.partial(three_terms_kernel, nt, nt * nc // 4, count, 2 * feats),
        out_shape=(
            jax.ShapeDtypeStruct((nt * WINDOW, width), F32),
            jax.ShapeDtypeStruct((nt, EXTRA, feats), F32),
        ),
        in_specs=[whole()] * 4,
        out_specs=(whole(), whole()),
        compiler_params=LARGE,
        cost_estimate=pl.CostEstimate(flops=flops, bytes_accessed=4 * nt * rows * width, transcendentals=0),
        name="three_terms",
    )(packed, gate_weight, up_weight, gate_other)
    blocks = pl.pallas_call(
        functools.partial(input_kernel, nt, feats, count),
        out_shape=jax.ShapeDtypeStruct((nt, nc, WINDOW, feats), BF16),
        in_specs=[whole(), whole(), whole(), whole(pl.ANY), whole()],
        out_specs=whole(pl.ANY),
        scratch_shapes=[
            pltpu.VMEM((SLOT, width), BF16),
            pltpu.VMEM((nt, nc, WINDOW, feats), BF16),
            pltpu.SemaphoreType.DMA(()),
            pltpu.SemaphoreType.DMA((nc // 2,)),
        ],
        compiler_params=LARGE,
        cost_estimate=pl.CostEstimate(flops=flops, bytes_accessed=6 * nt * rows * width, transcendentals=0),
        name="input_grad_blocks",
    )(packed, three, extras, up_other, tokens_all)
    blocks_sent = blocks.reshape(nt * nc, WINDOW, feats)
    blocks = lax.all_to_all(blocks_sent, ("tok", "col"), 0, 0, tiled=True)

    hidden_other = lax.ppermute(packed[:, 5 * SLOT :], "col", neighbours)
    down_cost = pl.CostEstimate(flops=flops // 2, bytes_accessed=3 * nt * rows * width, transcendentals=0)
    mine = pl.pallas_call(
        down_mine_kernel,
        out_shape=jax.ShapeDtypeStruct((count, width), F32),
        in_specs=[whole()] * 2,
        out_specs=whole(),
        compiler_params=LARGE,
        cost_estimate=down_cost,
        name="down_grads_mine",
    )(packed, grads_mine)
    d_down = pl.pallas_call(
        down_other_kernel,
        out_shape=jax.ShapeDtypeStruct((count, width), BF16),
        in_specs=[whole()] * 3,
        out_specs=whole(),
        compiler_params=LARGE,
        cost_estimate=down_cost,
        name="down_grads",
    )(hidden_other, grads_other, mine)

    d_tokens, d_gain = pl.pallas_call(
        functools.partial(final_kernel, model),
        out_shape=(
            jax.ShapeDtypeStruct((rows, feats), BF16),
            jax.ShapeDtypeStruct((1, feats), F32),
        ),
        in_specs=[whole()] * 4,
        out_specs=(whole(), whole()),
        compiler_params=SMALL,
        name="token_grads",
    )(blocks, tokens, d_out, gain_row)
    d_gain = d_gain.reshape(feats)
    return (d_tokens, d_gain, d_down)


def solution(mesh):
    placed = (
        P("tok", ("row", "col")),
        P("tok", ("row", "col")),
        P(("row", "col")),
        P(("tok", "col"), "row"),
        P(("tok", "col"), "row"),
        P(("tok", "col"), "row"),
    )
    return jax.shard_map(
        on_device,
        mesh=mesh,
        in_specs=placed,
        out_specs=(P("tok", ("row", "col")), P(("row", "col")), P(("tok", "col"), "row")),
        check_vma=False,
    )
```
